128 devices in a mesh: row: 8 (over z_hi, y), col: 16 (over x, z_lo, core).
Axes of the slice: x: 4, y: 4, z: 4 (z_hi: 2, z_lo: 2; z = z_hi * 2 + z_lo), core: 2. Of those that a mesh axis runs over, the one named last changes fastest.
Arguments:
- fine_qkv: bfloat16 [64, 256, 2304], P('row', 'col'), may hold values from -60 to 60
- merge_weight: bfloat16 [3072, 1536], replicated, may hold values from -0.109375 to 0.109375
- coarse_weight: bfloat16 [1536, 4608], P(None, 'col'), may hold values from -8 to 8
- norm_gain: float32 [1536], replicated, may hold values from 0.25 to 1.75
- cotangent: bfloat16 [32, 128, 1536], P('row', 'col'), may hold values from -6 to 6
Outputs:
- coarse_out: bfloat16 [32, 128, 1536], P('row', 'col')
- fine_grad: bfloat16 [64, 256, 2304], P('row', 'col')
The draws below stay inside these ranges and needn't reach their ends.
All inputs are finite; a program needn't handle non-finite values.
Results may differ from the reference program's by a relative error of at most 0.04.
Values may be sent and summed in bfloat16 or wider, within the bound.
A program may use at most 128 MiB of HBM per device.

```python
import math
import jax
import jax.numpy as jnp
from jax import lax

D1 = 768
D2 = 1536
HD = 64
FH = 64
FW = 256
CH = 32
CW = 128
N_ROW = 8


def draw_fine_qkv(key, part):
    key = jax.random.fold_in(key, 17)
    first_key = jax.random.fold_in(key, 0)
    shape = (FH, FW, 3 * D1)
    base = jnp.clip(jax.random.normal(first_key, shape, jnp.float32), -6.0, 6.0)
    return base.astype(jnp.bfloat16)


def draw_coarse_weight(key, part):
    key = jax.random.fold_in(key, 23)
    first_key = jax.random.fold_in(key, 0)
    base = jnp.clip(jax.random.normal(first_key, (D2, 3 * D2), jnp.float32), -6.0, 6.0) / math.sqrt(D2)
    return base.astype(jnp.bfloat16)


def level_of(stream_key, shape, cuts, smallest, top_value):
    def one(axis_at, parts):
        steps = jax.random.uniform(jax.random.fold_in(jax.random.fold_in(stream_key, 6), axis_at), (parts,), jnp.float32, smallest / len(cuts), top_value / len(cuts))
        return jnp.repeat(jnp.exp(steps), shape[axis_at] // parts).reshape((-1,) + (1,) * (len(shape) - axis_at - 1))

    factor_of = one(*cuts[0])
    for cut in cuts[1:]:
        factor_of = factor_of * one(*cut)
    return factor_of


def scatter_about(own_key, shape, spread, limit, shards=(), dtype=jnp.bfloat16):
    gain = level_of(own_key, shape, shards, -0.22, 0.18) if shards else 1.0
    entries = jax.random.normal(own_key, shape, jnp.float32) * spread * gain
    return jnp.minimum(jnp.maximum(entries, -limit), limit).astype(dtype)


def setup_inputs(seed: int = 0) -> dict:
    key_of = jax.random.split(jax.random.key(seed), 6)
    fine_qkv = draw_fine_qkv(jax.random.fold_in(key_of[5], 71), 0)
    merge_weight = scatter_about(key_of[1], (4 * D1, D2), (4 * D1) ** -0.5, 0.109375)
    coarse_weight = draw_coarse_weight(jax.random.fold_in(key_of[5], 71), 0)
    norm_gain = jnp.clip(1.0 + 0.15 * jax.random.normal(key_of[3], (D2,), jnp.float32), 0.25, 1.75)
    cotangent = scatter_about(key_of[4], (CH, CW, D2), 1.0, 6.0, ((0, 8), (1, 16)))
    return dict(fine_qkv=fine_qkv, merge_weight=merge_weight, coarse_weight=coarse_weight, norm_gain=norm_gain, cotangent=cotangent)


def neighbour_forward(query, keys_pad, valid, head_count):
    row_count, col_count, feat_width = query.shape
    head_size = feat_width // head_count
    score_scale = head_size ** (-0.5)
    query_wide = query.astype(jnp.float32).reshape(row_count, col_count, head_count, head_size)
    score_list = []
    for offset in range(49):
        off_row, off_col = divmod(offset, 7)
        keys = keys_pad[off_row:off_row + row_count, off_col:off_col + col_count, :feat_width]
        keys = keys.astype(jnp.float32).reshape(row_count, col_count, head_count, head_size)
        inside = valid[off_row:off_row + row_count, off_col:off_col + col_count][:, :, None]
        score_list.append(jnp.where(inside, lax.optimization_barrier(jnp.sum(query_wide * keys, -1)) * score_scale, -1e+30))
    scores = jnp.stack(score_list)
    highest = lax.optimization_barrier(jnp.max(scores, 0, keepdims=True))
    expd = jnp.exp(scores - highest)
    probs = expd / lax.optimization_barrier(jnp.sum(expd, 0, keepdims=True))
    output = jnp.zeros((row_count, col_count, head_count, head_size), jnp.float32)
    for offset in range(49):
        off_row, off_col = divmod(offset, 7)
        values = keys_pad[off_row:off_row + row_count, off_col:off_col + col_count, feat_width:]
        values = values.astype(jnp.float32).reshape(row_count, col_count, head_count, head_size)
        output = output + probs[offset][..., None] * values
    return (output.reshape(row_count, col_count, feat_width), probs)

def neighbour_backward(query, keys_pad, probs, grad_out, head_count):
    row_count, col_count, feat_width = query.shape
    head_size = feat_width // head_count
    score_scale = head_size ** (-0.5)
    query_wide = query.astype(jnp.float32).reshape(row_count, col_count, head_count, head_size)
    grad_wide = grad_out.astype(jnp.float32).reshape(row_count, col_count, head_count, head_size)
    grad_list = []
    for offset in range(49):
        off_row, off_col = divmod(offset, 7)
        values = keys_pad[off_row:off_row + row_count, off_col:off_col + col_count, feat_width:]
        values = values.astype(jnp.float32).reshape(row_count, col_count, head_count, head_size)
        grad_list.append(lax.optimization_barrier(jnp.sum(grad_wide * values, -1)))
    grad_probs = jnp.stack(grad_list)
    delta = lax.optimization_barrier(jnp.sum(probs * grad_probs, 0))
    grad_query = jnp.zeros_like(query_wide)
    grad_pad = jnp.zeros(keys_pad.shape, jnp.float32)
    for offset in range(49):
        off_row, off_col = divmod(offset, 7)
        keys = keys_pad[off_row:off_row + row_count, off_col:off_col + col_count, :feat_width]
        keys = keys.astype(jnp.float32).reshape(row_count, col_count, head_count, head_size)
        grad_scores = probs[offset] * (grad_probs[offset] - delta)
        grad_query = grad_query + grad_scores[..., None] * keys
        key_part = (grad_scores[..., None] * query_wide * score_scale).reshape(row_count, col_count, feat_width)
        value_part = (probs[offset][..., None] * grad_wide).reshape(row_count, col_count, feat_width)
        grad_pad = grad_pad.at[off_row:off_row + row_count, off_col:off_col + col_count].add(jnp.concatenate([key_part, value_part], -1))
    return ((grad_query * score_scale).reshape(row_count, col_count, feat_width), grad_pad)

def merge_tiles(fine):
    row_count, col_count, feat_width = fine.shape
    merged = fine.reshape(row_count // 2, 2, col_count // 2, 2, feat_width).transpose(0, 2, 1, 3, 4)
    return merged.reshape(row_count // 2, col_count // 2, 4 * feat_width)

def split_tiles(coarse):
    row_count, col_count, feat_width = coarse.shape
    fine = coarse.reshape(row_count, col_count, 2, 2, feat_width // 4).transpose(0, 2, 1, 3, 4)
    return fine.reshape(2 * row_count, 2 * col_count, feat_width // 4)

def norm_forward(coarse, norm_gain):
    wide = coarse.astype(jnp.float32)
    inverse = lax.rsqrt(lax.optimization_barrier(jnp.mean(wide * wide, -1, keepdims=True)) + 1e-06)
    return (wide * inverse * norm_gain).astype(jnp.bfloat16)

def norm_backward(coarse, norm_gain, grad_normed):
    wide = coarse.astype(jnp.float32)
    inverse = lax.rsqrt(lax.optimization_barrier(jnp.mean(wide * wide, -1, keepdims=True)) + 1e-06)
    scaled = grad_normed.astype(jnp.float32) * norm_gain
    return inverse * (scaled - wide * inverse * inverse * lax.optimization_barrier(jnp.mean(scaled * wide, -1, keepdims=True)))

def group_attention(coarse_qkv, grad_out):
    token_count = coarse_qkv.shape[0]
    feat_width = coarse_qkv.shape[1] // 3
    head_count = feat_width // HD
    score_scale = HD ** (-0.5)
    wide = coarse_qkv.astype(jnp.float32)
    query = wide[:, :feat_width].reshape(token_count, head_count, HD)
    keys = wide[:, feat_width:2 * feat_width].reshape(token_count, head_count, HD)
    values = wide[:, 2 * feat_width:].reshape(token_count, head_count, HD)
    scores = jnp.einsum('qhd,khd->hqk', query, keys) * score_scale
    highest = lax.optimization_barrier(jnp.max(scores, -1, keepdims=True))
    expd = jnp.exp(scores - highest)
    probs = expd / lax.optimization_barrier(jnp.sum(expd, -1, keepdims=True))
    output = jnp.einsum('hqk,khd->qhd', probs, values)
    grad_wide = grad_out.astype(jnp.float32).reshape(token_count, head_count, HD)
    grad_probs = jnp.einsum('qhd,khd->hqk', grad_wide, values)
    delta = jnp.einsum('qhd,qhd->hq', grad_wide, output)
    grad_scores = probs * (grad_probs - delta[:, :, None])
    grad_query = jnp.einsum('hqk,khd->qhd', grad_scores, keys) * score_scale
    grad_keys = jnp.einsum('hqk,qhd->khd', grad_scores, query) * score_scale
    grad_values = jnp.einsum('hqk,qhd->khd', probs, grad_wide)
    grads = jnp.concatenate([grad_query.reshape(token_count, feat_width), grad_keys.reshape(token_count, feat_width), grad_values.reshape(token_count, feat_width)], -1)
    return (output.reshape(token_count, feat_width), grads)

def reference(fine_qkv, merge_weight, coarse_weight, norm_gain, cotangent):
    fine_rows, fine_cols, triple = fine_qkv.shape
    fine_width = triple // 3
    query = fine_qkv[..., :fine_width]
    keys_pad = jnp.pad(fine_qkv[..., fine_width:], ((3, 3), (3, 3), (0, 0)))
    valid = jnp.pad(jnp.ones((fine_rows, fine_cols), bool), 3)
    attended, probs = neighbour_forward(query, keys_pad, valid, fine_width // HD)
    attended = attended.astype(jnp.bfloat16)
    merged = merge_tiles(attended)
    coarse_rows, coarse_cols, merged_width = merged.shape
    coarse = jnp.dot(merged.reshape(-1, merged_width), merge_weight, preferred_element_type=jnp.float32).astype(jnp.bfloat16)
    normed = norm_forward(coarse, norm_gain)
    coarse_qkv = jnp.dot(normed, coarse_weight, preferred_element_type=jnp.float32).astype(jnp.bfloat16)
    coarse_width = coarse.shape[1]
    qkv_groups = coarse_qkv.reshape(N_ROW, -1, 3 * coarse_width)
    cot_groups = cotangent.reshape(N_ROW, -1, coarse_width)
    outputs, grads = lax.map(lambda pair: group_attention(pair[0], pair[1]), (qkv_groups, cot_groups))
    coarse_out = outputs.reshape(coarse_rows, coarse_cols, coarse_width).astype(jnp.bfloat16)
    qkv_grad = grads.reshape(-1, 3 * coarse_width).astype(jnp.bfloat16)
    normed_grad = lax.dot_general(qkv_grad, coarse_weight, (((1,), (1,)), ((), ())), preferred_element_type=jnp.float32).astype(jnp.bfloat16)
    coarse_grad = norm_backward(coarse, norm_gain, normed_grad).astype(jnp.bfloat16)
    merged_grad = lax.dot_general(coarse_grad, merge_weight, (((1,), (1,)), ((), ())), preferred_element_type=jnp.float32).astype(jnp.bfloat16)
    attended_grad = split_tiles(merged_grad.reshape(coarse_rows, coarse_cols, merged_width))
    query_grad, pad_grad = neighbour_backward(query, keys_pad, probs, attended_grad, fine_width // HD)
    fine_grad = jnp.concatenate([query_grad, pad_grad[3:-3, 3:-3]], -1).astype(jnp.bfloat16)
    return (coarse_out, fine_grad)
```

```python
import functools

import jax
import jax.numpy as jnp
from jax import lax
from jax.experimental import pallas as pl
from jax.experimental.pallas import tpu as pltpu
from jax.sharding import PartitionSpec as P

MESH = pl.DeviceIdType.MESH
BF = jnp.bfloat16
F32 = jnp.float32
HD = 64
SCALE = HD ** (-0.5)
NEG = -1e30

OWN, SLAB = 128, 352
UP, DOWN, LEFT, RIGHT, UL, UR, DL, DR = (
    (128, 48), (176, 48), (224, 32), (256, 32), (288, 16), (304, 16), (320, 16), (336, 16),
)


def iotas(shape):
    return lax.broadcasted_iota(jnp.int32, shape, 0), lax.broadcasted_iota(jnp.int32, shape, 1)


def pick(index, other):
    return jnp.where(index == other, 1.0, 0.0).astype(BF)


def pack_token(i):
    j = i & 31
    strip_col = j >> 3
    strip = (j & 7) * 16 + strip_col + jnp.where(i >= 32, 13, 0)
    strip = jnp.where(strip_col < 3, strip, -1)
    j = i & 15
    k = (i - 64) >> 4
    col, row = j >> 2, j & 3
    corner = (row + jnp.where(k >= 2, 5, 0)) * 16 + col + (k & 1) * 13
    corner = jnp.where(jnp.maximum(row, col) < 3, corner, -1)
    return jnp.where(i < 64, strip, corner)


def merge_token(i):
    t, s = i & 31, i >> 5
    return (2 * (t >> 3) + (s >> 1)) * 16 + 2 * (t & 7) + (s & 1)


def window_bias(up_ok, down_ok, left_ok, right_ok):
    i, lane = iotas((SLAB, 128))
    query_row, query_col = lane >> 4, lane & 15
    far = 1000
    j = i - 128
    edge_row = (j >> 4) + jnp.where(i < 176, -3, 5)
    edge_row = jnp.where(jnp.where(i < 176, up_ok, down_ok) > 0, edge_row, far)
    j = (i - 224) & 31
    strip_col = j >> 3
    strip_ok = jnp.where(i < 256, left_ok, right_ok) * jnp.where(strip_col < 3, 1, 0)
    strip_row = jnp.where(strip_ok > 0, j & 7, far)
    strip_col = strip_col + jnp.where(i < 256, -3, 16)
    j, k = (i - 288) & 15, (i - 288) >> 4
    col, row = j >> 2, j & 3
    corner_ok = jnp.where(k < 2, up_ok, down_ok) * jnp.where((k & 1) == 0, left_ok, right_ok)
    corner_ok = corner_ok * jnp.where(jnp.maximum(row, col) < 3, 1, 0)
    corner_row = jnp.where(corner_ok > 0, row + jnp.where(k < 2, -3, 8), far)
    corner_col = col + jnp.where((k & 1) == 0, -3, 16)
    key_row = jnp.where(
        i < 128, i >> 4, jnp.where(i < 224, edge_row, jnp.where(i < 288, strip_row, corner_row))
    )
    key_col = jnp.where(i < 224, i & 15, jnp.where(i < 288, strip_col, corner_col))
    gap = jnp.maximum(jnp.abs(key_row - query_row), jnp.abs(key_col - query_col))
    return jnp.where(gap <= 3, 0.0, NEG)


def dot(a, b):
    return jnp.dot(a, b, preferred_element_type=F32)


def dot_nt(a, b):
    return lax.dot_general(a, b, (((1,), (1,)), ((), ())), preferred_element_type=F32)


def dot_tn(a, b):
    return lax.dot_general(a, b, (((0,), (0,)), ((), ())), preferred_element_type=F32)


def softmax_rows(scores):
    highest = jnp.max(scores, 0, keepdims=True)
    expd = jnp.exp(scores - highest)
    return expd * (1.0 / jnp.sum(expd, 0, keepdims=True))


def kernel(
    rows, cols,
    fine, mw_hbm, cw, gain, cot,
    co_out, fg_out,
    mw, slab, pack, bias, probs, dscore, att, xm, coarse,
    wsh, wpart, w6, nb, cotp, gt, qbuf, kslab, vslab, dsend, drecv, dqkv, osend, corecv,
    ngs, rs, mg, gown, gsend, gr,
    mw_sem, hs, hr, gs, grs, ws, wr, wps, wpr, wfs, wfr, as_, ar, cs, cr, ks, kr, ds_, dr_, os_, orr, rss, rsr,
):
    row, col = lax.axis_index("row"), lax.axis_index("col")
    chip, core = col // 2, col % 2
    chips = cols // 2
    up, down = (row + rows - 1) % rows, (row + 1) % rows
    left, right = (col + cols - 1) % cols, (col + 1) % cols
    partner = col + 1 - 2 * core
    group, member = col // 4, col % 4

    def remote(src, dst, send, recv, to_row, to_col):
        return pltpu.make_async_remote_copy(
            src_ref=src, dst_ref=dst, send_sem=send, recv_sem=recv,
            device_id=(to_row, to_col), device_id_type=MESH,
        )

    barrier = pltpu.get_barrier_semaphore()
    for step in range(1, cols):
        pl.semaphore_signal(barrier, inc=1, device_id=(row, (col + step) % cols), device_id_type=MESH)
    for to_row in (up, down):
        for to_col in (left, col, right):
            pl.semaphore_signal(barrier, inc=1, device_id=(to_row, to_col), device_id_type=MESH)

    load = pltpu.make_async_copy(mw_hbm, mw, mw_sem)
    load.start()

    i, t = iotas((128, 128))
    pack[...] = dot(pick(pack_token(i), t), fine[:, 768:2304]).astype(BF)
    for c in range(chips):
        cotp[c, :, 0:128] = cot[:, 128 * c : 128 * c + 128]
        tile = 1024 + 128 * (c // 2)
        cotp[c, :, 128:256] = cot[:, tile : tile + 128]

    pl.semaphore_wait(barrier, cols + 5)

    def part(ref, block):
        return ref.at[pl.ds(block[0], block[1])]

    halo = [
        (fine.at[pl.ds(0, 48), pl.ds(768, 1536)], DOWN, up, col),
        (fine.at[pl.ds(80, 48), pl.ds(768, 1536)], UP, down, col),
        (pack.at[pl.ds(0, 32)], RIGHT, row, left),
        (pack.at[pl.ds(32, 32)], LEFT, row, right),
        (pack.at[pl.ds(64, 16)], DR, up, left),
        (pack.at[pl.ds(80, 16)], DL, up, right),
        (pack.at[pl.ds(96, 16)], UR, down, left),
        (pack.at[pl.ds(112, 16)], UL, down, right),
    ]
    halo = [
        remote(src, part(slab, block), hs.at[n], hr.at[n], to_row, to_col)
        for n, (src, block, to_row, to_col) in enumerate(halo)
    ]
    for copy in halo:
        copy.start()

    i, t = iotas((288, 384))
    shift = jnp.where(t - i == 32 * member, 1.0, 0.0).astype(BF)
    for n in range(6):
        moved = dot(cw[256 * n : 256 * n + 256, :], shift).astype(BF)
        for k in range(3):
            wsh[k, 256 * n : 256 * n + 256, :] = moved[:, 128 * k : 128 * k + 128]
    tail = remote(wsh.at[2], wpart, wps, wpr, row, right)

    @pl.when(member < 3)
    def _():
        tail.start()

    cot_copies = [
        remote(cotp.at[(chip + d) % chips], gt.at[d], cs.at[d], cr.at[d], row, 2 * ((chip + d) % chips) + core)
        for d in range(1, chips)
    ]
    for copy in cot_copies:
        copy.start()
    gt[0] = cotp[chip]

    slab[0:OWN, :] = fine[:, 768:2304]
    window = window_bias(
        jnp.where(row > 0, 1, 0), jnp.where(row < rows - 1, 1, 0),
        jnp.where(col > 0, 1, 0), jnp.where(col < cols - 1, 1, 0),
    )
    bias[:, 0:128] = window
    bias[:, 128:256] = window
    lane = lax.broadcasted_iota(jnp.int32, (1, 128), 1)
    even = jnp.where(lane < 64, 1.0, 0.0).astype(BF)
    odd = jnp.where(lane < 64, 0.0, 1.0).astype(BF)
    _, lanes = iotas((128, 128))

    def both_heads(block):
        return jnp.concatenate([block * even, block * odd], 0)

    def own_lanes(two):
        return jnp.where(lanes < 64, two[0:128], two[128:256])

    for copy in halo:
        copy.wait_recv()

    def fine_pair(p):
        at = 128 * p
        query = both_heads(fine[:, at : at + 128] * SCALE)
        scores = dot_nt(slab[:, at : at + 128], query) + bias[...]
        weights = softmax_rows(scores).astype(BF)
        probs[p] = weights
        out = dot_tn(weights, slab[:, 768 + at : 768 + at + 128])
        att[:, at : at + 128] = own_lanes(out).astype(BF)

    def tile_routes(k):
        tile = 9 * group + 2 * member + k
        kind, pair = tile // 12, tile % 12
        single = jnp.where(pair >= 8, 1, 0)
        first = jnp.where(pair >= 8, 4 * (pair - 8) + 1, 2 * pair)
        second = 4 * (pair - 8) + 3
        have = (member == 3) if k == 2 else (member >= 0)
        return [
            (have, first, single, kind, ws.at[2 * k]),
            (have & (pair >= 8), second, single, kind, ws.at[2 * k + 1]),
        ]

    def send_tiles():
        @pl.when(member > 0)
        def _():
            tail.wait_recv()
            wsh[0] = wsh[0] + wpart[...]

        for k in range(3):
            for have, to, single, kind, sem in tile_routes(k):

                @pl.when(have & (to != col))
                def _():
                    remote(wsh.at[k], w6.at[single, kind], sem, wr.at[kind], row, to).start()

                @pl.when(have & (to == col))
                def _():
                    w6[single, kind] = wsh[k]

    for p in range(6):
        fine_pair(p)
        if p == 2:
            send_tiles()

    i, t = iotas((128, 128))
    xm[...] = dot(pick(merge_token(i), t), att[...]).astype(BF)
    load.wait()

    def merge_step(n, _):
        at = pl.ds(pl.multiple_of(256 * n, 256), 256)
        total = dot(xm[0:32, :], mw[0:768, at])
        for s in range(1, 4):
            total = total + dot(xm[32 * s : 32 * s + 32, :], mw[768 * s : 768 * s + 768, at])
        coarse[:, at] = total.astype(BF)
        return 0

    lax.fori_loop(0, 6, merge_step, 0)
    wide = coarse[...].astype(F32)
    inverse = lax.rsqrt(jnp.mean(wide * wide, -1, keepdims=True) + 1e-06)
    nb[0] = (wide * inverse * gain[...]).astype(BF)
    gather = [
        remote(nb.at[0], nb.at[d], as_.at[d], ar.at[d], row, 2 * ((chip + d) % chips) + core)
        for d in range(1, chips)
    ]
    for copy in gather:
        copy.start()

    forward = []
    for kind in range(3):
        tile = 12 * kind + jnp.where(core == 0, chip, 8 + chip // 2)
        source = 4 * (tile // 9) + jnp.minimum((tile % 9) // 2, 3)
        slot = w6.at[core, kind]

        @pl.when(source != col)
        def _():
            remote(slot, slot, ws.at[0], wr.at[kind], row, partner).wait_recv()

        copy = remote(slot, slot, wfs.at[kind], wfr.at[kind], row, partner)
        copy.start()
        forward.append(copy)
    for kind in range(3):
        slot = w6.at[1 - core, kind]
        remote(slot, slot, wfs.at[kind], wfr.at[kind], row, partner).wait_recv()
    for copy in gather:
        copy.wait_recv()

    tokens = 32 * chips
    normed = nb[...].reshape(tokens, 1536)

    def project(kind):
        return dot(normed, jnp.concatenate([w6[0, kind], w6[1, kind]], 1)).astype(BF)

    kslab[0:tokens, :] = project(1)
    swap_k = remote(kslab.at[pl.ds(0, tokens)], kslab.at[pl.ds(tokens, tokens)], ks.at[0], kr.at[0], row, partner)
    swap_k.start()
    vslab[0:tokens, :] = project(2)
    swap_v = remote(vslab.at[pl.ds(0, tokens)], vslab.at[pl.ds(tokens, tokens)], ks.at[1], kr.at[1], row, partner)
    swap_v.start()
    qbuf[...] = project(0)
    for copy in cot_copies:
        copy.wait_recv()
    swap_k.wait_recv()
    swap_v.wait_recv()

    alone = jnp.where((lane >> 6) == chip % 2, 1.0, 0.0)
    grads = gt[...].reshape(tokens, 256)
    outs, dqs, dks, dvs = [], [], [], []
    for head in range(3):
        at = 128 * (head // 2)
        mask = (even, odd, alone.astype(BF))[head]
        query = qbuf[:, at : at + 128] * mask * SCALE
        grad = grads[:, at : at + 128] * mask
        keys, values = kslab[:, at : at + 128], vslab[:, at : at + 128]
        weights = softmax_rows(dot_nt(keys, query))
        weights_low = weights.astype(BF)
        outs.append(dot_tn(weights_low, values))
        dp = dot_nt(values, grad)
        delta = jnp.sum(weights * dp, 0, keepdims=True)
        dscores = (weights * (dp - delta)).astype(BF)
        dqs.append(dot_tn(dscores, keys) * SCALE)
        dks.append(dot(dscores, query))
        dvs.append(dot(weights_low, grad))
    for which, parts in enumerate((dks, dvs)):
        both = jnp.concatenate([parts[0] + parts[1], parts[2]], 1)
        dsend[which] = both[tokens:].astype(BF)
        dqkv[:, 256 + 256 * which : 512 + 256 * which] = both[0:tokens].astype(BF)
    swap_d = remote(dsend, drecv, ds_, dr_, row, partner)
    swap_d.start()
    wide_lane = lax.broadcasted_iota(jnp.int32, (tokens, 128), 1)
    dqkv[:, 0:128] = jnp.where(wide_lane < 64, dqs[0], dqs[1]).astype(BF)
    dqkv[:, 128:256] = (dqs[2] * alone).astype(BF)
    out = jnp.concatenate([jnp.where(wide_lane < 64, outs[0], outs[1]), outs[2] * alone], 1)
    osend[...] = out.astype(BF).reshape(chips, 32, 256)
    corecv[chip] = osend[0]
    out_copies = [
        remote(osend.at[d], corecv.at[chip], os_.at[d], orr.at[d], row, 2 * ((chip + chips - d) % chips) + core)
        for d in range(1, chips)
    ]
    swap_d.wait_recv()
    for which in range(2):
        at = 256 + 256 * which
        dqkv[:, at : at + 256] = (dqkv[:, at : at + 256].astype(F32) + drecv[which].astype(F32)).astype(BF)

    def back_step(n, _):
        at = pl.ds(pl.multiple_of(256 * n, 256), 256)
        weight = jnp.concatenate([w6[half, kind, at, :] for kind in range(3) for half in range(2)], 1)
        ngs[:, :, at] = dot_nt(dqkv[...], weight).astype(BF).reshape(chips, 32, 256)
        return 0

    lax.fori_loop(0, 6, back_step, 0)
    scatter = [
        remote(ngs.at[d], rs.at[d], rss.at[d], rsr.at[d], row, 2 * ((chip + chips - d) % chips) + core)
        for d in range(1, chips)
    ]
    for copy in scatter:
        copy.start()
    for copy in out_copies:
        copy.start()
    total = ngs[0].astype(F32)
    for d in range(1, chips):
        scatter[d - 1].wait_recv()
        total = total + rs[d].astype(F32)

    wide = coarse[...].astype(F32)
    inverse = lax.rsqrt(jnp.mean(wide * wide, -1, keepdims=True) + 1e-06)
    scaled = total * gain[...]
    cgrad = inverse * (scaled - wide * (inverse * inverse * jnp.mean(scaled * wide, -1, keepdims=True)))
    xg = cgrad.astype(BF)
    nb_grad = xg

    def unmerge_step(n, _):
        weight = mw[pl.ds(pl.multiple_of(256 * n, 256), 256), :]
        part_grad = dot_nt(nb_grad, weight).astype(BF)
        s, at = n // 3, pl.multiple_of(256 * (n % 3), 256)
        mg[pl.ds(pl.multiple_of(32 * s, 32), 32), pl.ds(at, 256)] = part_grad
        return 0

    lax.fori_loop(0, 12, unmerge_step, 0)
    i, t = iotas((128, 128))
    agrad = dot(pick(merge_token(t), i), mg[...]).astype(BF)

    for p in range(6):
        at = 128 * p
        query = both_heads(fine[:, at : at + 128] * SCALE)
        grad = both_heads(agrad[:, at : at + 128])
        weights_low = probs[p]
        weights = weights_low.astype(F32)
        dp = dot_nt(slab[:, 768 + at : 768 + at + 128], grad)
        delta = jnp.sum(weights * dp, 0, keepdims=True)
        ds_low = (weights * (dp - delta)).astype(BF)
        dscore[p] = ds_low
        gsend[:, at : at + 128] = dot(ds_low[OWN:], query).astype(BF)
        gsend[:, 768 + at : 768 + at + 128] = dot(weights_low[OWN:], grad).astype(BF)
    back = [
        (UP, 48, up, col), (DOWN, 0, down, col), (LEFT, 128, row, left), (RIGHT, 96, row, right),
        (UL, 208, up, left), (UR, 192, up, right), (DL, 176, down, left), (DR, 160, down, right),
    ]
    back = [
        remote(
            gsend.at[pl.ds(block[0] - OWN, block[1])], gr.at[pl.ds(to, block[1])],
            gs.at[n], grs.at[n], to_row, to_col,
        )
        for n, (block, to, to_row, to_col) in enumerate(back)
    ]
    for copy in back:
        copy.start()
    for p in range(6):
        at = 128 * p
        query = both_heads(fine[:, at : at + 128] * SCALE)
        grad = both_heads(agrad[:, at : at + 128])
        gown[:, at : at + 128] = dot(dscore[p, 0:OWN, :], query)
        gown[:, 768 + at : 768 + at + 128] = dot(probs[p, 0:OWN, :], grad)
        dq = dot_tn(dscore[p], slab[:, at : at + 128]) * SCALE
        fg_out[:, at : at + 128] = own_lanes(dq).astype(BF)

    for d in range(1, chips):
        source = (chip + d) % chips
        remote(osend.at[d], corecv.at[source], os_.at[d], orr.at[d], row, 2 * source + core).wait_recv()
    for c in range(chips):
        co_out[:, 128 * c : 128 * c + 128] = corecv[c, :, 0:128]
    for c in range(0, chips, 2):
        at = 1024 + 64 * c
        co_out[:, at : at + 128] = corecv[c, :, 128:256] + corecv[c + 1, :, 128:256]

    for copy in back:
        copy.wait_recv()
    i, t = iotas((128, 128))
    pulled = dot(pick(pack_token(t), i), gr[96:224, :])
    kv_grad = gown[...] + pulled
    fg_out[48:80, 768:2304] = kv_grad[48:80].astype(BF)
    fg_out[0:48, 768:2304] = (kv_grad[0:48] + gr[0:48, :].astype(F32)).astype(BF)
    fg_out[80:128, 768:2304] = (kv_grad[80:128] + gr[48:96, :].astype(F32)).astype(BF)

    for copy in halo + cot_copies + gather + forward + [swap_k, swap_v, swap_d] + out_copies + scatter + back:
        copy.wait_send()

    @pl.when(member < 3)
    def _():
        tail.wait_send()

    for k in range(3):
        for have, to, single, kind, sem in tile_routes(k):

            @pl.when(have & (to != col))
            def _():
                remote(wsh.at[k], w6.at[single, kind], sem, wr.at[kind], row, to).wait_send()


def shards(mesh_rows, mesh_cols, fine_qkv, merge_weight, coarse_weight, norm_gain, cotangent):
    chips = mesh_cols // 2
    tokens = 32 * chips
    vmem = pl.BlockSpec(memory_space=pltpu.VMEM)
    dma = pltpu.SemaphoreType.DMA

    def low(*shape):
        return pltpu.VMEM(shape, BF)

    def full(*shape):
        return pltpu.VMEM(shape, F32)

    coarse_out, fine_grad = pl.pallas_call(
        functools.partial(kernel, mesh_rows, mesh_cols),
        out_shape=(jax.ShapeDtypeStruct((32, 1536), BF), jax.ShapeDtypeStruct((128, 2304), BF)),
        in_specs=[vmem, pl.BlockSpec(memory_space=pl.ANY), vmem, vmem, vmem],
        out_specs=(vmem, vmem),
        scratch_shapes=[
            low(3072, 1536), low(SLAB, 1536), low(128, 1536), full(SLAB, 256), low(6, SLAB, 256),
            low(6, SLAB, 256), low(128, 768), low(128, 768), low(32, 1536),
            low(3, 1536, 128), low(1536, 128), low(2, 3, 1536, 128), low(chips, 32, 1536),
            low(chips, 32, 256), low(chips, 32, 256), low(tokens, 256), low(2 * tokens, 256),
            low(2 * tokens, 256), low(2, tokens, 256), low(2, tokens, 256), low(tokens, 768),
            low(chips, 32, 256), low(chips, 32, 256),
            low(chips, 32, 1536), low(chips, 32, 1536), low(128, 768), full(128, 1536),
            low(224, 1536), low(224, 1536),
            dma, dma((8,)), dma((8,)), dma((8,)), dma((8,)), dma((6,)), dma((3,)), dma, dma,
            dma((3,)), dma((3,)), dma((chips,)), dma((chips,)), dma((chips,)), dma((chips,)),
            dma((2,)), dma((2,)), dma, dma, dma((chips,)), dma((chips,)), dma((chips,)), dma((chips,)),
        ],
        compiler_params=pltpu.CompilerParams(
            collective_id=0, has_side_effects=True, vmem_limit_bytes=56 * 1024 * 1024
        ),
    )(
        fine_qkv.reshape(128, 2304),
        merge_weight,
        coarse_weight,
        norm_gain.reshape(1, 1536),
        cotangent.reshape(32, 1536),
    )
    return coarse_out.reshape(4, 8, 1536), fine_grad.reshape(8, 16, 2304)


def solution(mesh):
    placed = (P("row", "col", None), P(), P(None, "col"), P(), P("row", "col", None))
    return jax.shard_map(
        functools.partial(shards, mesh.shape["row"], mesh.shape["col"]),
        mesh=mesh,
        in_specs=placed,
        out_specs=(P("row", "col", None), P("row", "col", None)),
        check_vma=False,
    )
```

```python
import functools

import jax
import jax.numpy as jnp
from jax import lax
from jax.experimental import pallas as pl
from jax.experimental.pallas import tpu as pltpu
from jax.sharding import PartitionSpec as P

MESH = pl.DeviceIdType.MESH
BF = jnp.bfloat16
F32 = jnp.float32
HD = 64
SCALE = HD ** (-0.5)
NEG = -1e30

OWN, SLAB = 128, 352
UP, DOWN, LEFT, RIGHT, UL, UR, DL, DR = (
    (128, 48), (176, 48), (224, 32), (256, 32), (288, 16), (304, 16), (320, 16), (336, 16),
)


def iotas(shape):
    return lax.broadcasted_iota(jnp.int32, shape, 0), lax.broadcasted_iota(jnp.int32, shape, 1)


def pick(index, other):
    return jnp.where(index == other, 1.0, 0.0).astype(BF)


def pack_token(i):
    j = i & 31
    strip_col = j >> 3
    strip = (j & 7) * 16 + strip_col + jnp.where(i >= 32, 13, 0)
    strip = jnp.where(strip_col < 3, strip, -1)
    j = i & 15
    k = (i - 64) >> 4
    col, row = j >> 2, j & 3
    corner = (row + jnp.where(k >= 2, 5, 0)) * 16 + col + (k & 1) * 13
    corner = jnp.where(jnp.maximum(row, col) < 3, corner, -1)
    return jnp.where(i < 64, strip, corner)


def merge_token(i):
    t, s = i & 31, i >> 5
    return (2 * (t >> 3) + (s >> 1)) * 16 + 2 * (t & 7) + (s & 1)


def window_bias(up_ok, down_ok, left_ok, right_ok):
    i, lane = iotas((SLAB, 128))
    query_row, query_col = lane >> 4, lane & 15
    far = 1000
    j = i - 128
    edge_row = (j >> 4) + jnp.where(i < 176, -3, 5)
    edge_row = jnp.where(jnp.where(i < 176, up_ok, down_ok) > 0, edge_row, far)
    j = (i - 224) & 31
    strip_col = j >> 3
    strip_ok = jnp.where(i < 256, left_ok, right_ok) * jnp.where(strip_col < 3, 1, 0)
    strip_row = jnp.where(strip_ok > 0, j & 7, far)
    strip_col = strip_col + jnp.where(i < 256, -3, 16)
    j, k = (i - 288) & 15, (i - 288) >> 4
    col, row = j >> 2, j & 3
    corner_ok = jnp.where(k < 2, up_ok, down_ok) * jnp.where((k & 1) == 0, left_ok, right_ok)
    corner_ok = corner_ok * jnp.where(jnp.maximum(row, col) < 3, 1, 0)
    corner_row = jnp.where(corner_ok > 0, row + jnp.where(k < 2, -3, 8), far)
    corner_col = col + jnp.where((k & 1) == 0, -3, 16)
    key_row = jnp.where(
        i < 128, i >> 4, jnp.where(i < 224, edge_row, jnp.where(i < 288, strip_row, corner_row))
    )
    key_col = jnp.where(i < 224, i & 15, jnp.where(i < 288, strip_col, corner_col))
    gap = jnp.maximum(jnp.abs(key_row - query_row), jnp.abs(key_col - query_col))
    return jnp.where(gap <= 3, 0.0, NEG)


def dot(a, b):
    return jnp.dot(a, b, preferred_element_type=F32)


def dot_nt(a, b):
    return lax.dot_general(a, b, (((1,), (1,)), ((), ())), preferred_element_type=F32)


def dot_tn(a, b):
    return lax.dot_general(a, b, (((0,), (0,)), ((), ())), preferred_element_type=F32)


def softmax_rows(scores):
    highest = jnp.max(scores, 0, keepdims=True)
    expd = jnp.exp(scores - highest)
    return expd * (1.0 / jnp.sum(expd, 0, keepdims=True))


def phase(name, work):
    work()


def kernel(
    rows, cols,
    fine_hbm, mw_hbm, cw_hbm, gain_hbm, cot_hbm,
    co_out, fg_out,
    fine, cot, gain_flat, mw, slab, pack, bias, probs, dscore, att, xm,
    w, nb, normed, cotp, gt, qbuf, kslab, vslab, pbuf, dsbuf, dsend, drecv, dqkv, osend, corecv,
    ngs, rs, mg, ag, gown, gsend, gr,
    fine_sem, cot_sem, gain_sem, mw_sem, hs, hr, gs, grs, ws, wr, wys, wfs, as_, ar, cs, cr, ks, kr, ds_, dr_, os_, orr, rss, rsr,
):
    row, col = lax.axis_index("row"), lax.axis_index("col")
    chip, core = col // 2, col % 2
    chips = cols // 2
    tokens = 32 * chips
    up, down = (row + rows - 1) % rows, (row + 1) % rows
    left, right = (col + cols - 1) % cols, (col + 1) % cols
    partner = col + 1 - 2 * core
    high, low_row = row // 4, row % 4
    ring = [4 * high + (low_row + j) % 4 for j in range(1, 4)]

    def remote(src, dst, send, recv, to_row, to_col):
        return pltpu.make_async_remote_copy(
            src_ref=src, dst_ref=dst, send_sem=send, recv_sem=recv,
            device_id=(to_row, to_col), device_id_type=MESH,
        )

    def part(ref, block):
        return ref.at[pl.ds(block[0], block[1])]

    barrier = pltpu.get_barrier_semaphore()
    for step in range(1, cols):
        pl.semaphore_signal(barrier, inc=1, device_id=(row, (col + step) % cols), device_id_type=MESH)
    for to_row in (up, down):
        for to_col in (left, col, right):
            pl.semaphore_signal(barrier, inc=1, device_id=(to_row, to_col), device_id_type=MESH)
    for to_row in ring:
        pl.semaphore_signal(barrier, inc=1, device_id=(to_row, col), device_id_type=MESH)

    load_fine = pltpu.make_async_copy(fine_hbm, fine, fine_sem)
    load_fine.start()
    load_cot = pltpu.make_async_copy(cot_hbm, cot, cot_sem)
    load_cot.start()
    load_gain = pltpu.make_async_copy(gain_hbm, gain_flat, gain_sem)
    load_gain.start()
    load = pltpu.make_async_copy(mw_hbm, mw, mw_sem)
    load.start()

    lane = lax.broadcasted_iota(jnp.int32, (1, 128), 1)
    even = jnp.where(lane < 64, 1.0, 0.0).astype(BF)
    odd = jnp.where(lane < 64, 0.0, 1.0).astype(BF)
    _, lanes = iotas((128, 128))

    def pack_all():
        i, t = iotas((128, 128))
        pack[...] = dot(pick(pack_token(i), t), fine[:, 768:2304]).astype(BF)
        for c in range(chips):
            cotp[c, :, 0:128] = cot[:, 128 * c : 128 * c + 128]
            at = 1024 + 64 * c
            cotp[c, :, 128:256] = jnp.concatenate([cot[:, at : at + 64], jnp.zeros((32, 64), BF)], 1)
        for kind in range(3):
            w[kind, 6:8] = jnp.zeros((2, 32, 1536), BF)

    load_fine.wait()
    load_cot.wait()
    load_gain.wait()
    gain = gain_flat[...].reshape(1, 1536)
    phase("pack", pack_all)

    pl.semaphore_wait(barrier, cols + 8)

    halo = [
        (fine.at[pl.ds(0, 48), pl.ds(768, 1536)], DOWN, up, col),
        (fine.at[pl.ds(80, 48), pl.ds(768, 1536)], UP, down, col),
        (pack.at[pl.ds(0, 32)], RIGHT, row, left),
        (pack.at[pl.ds(32, 32)], LEFT, row, right),
        (pack.at[pl.ds(64, 16)], DR, up, left),
        (pack.at[pl.ds(80, 16)], DL, up, right),
        (pack.at[pl.ds(96, 16)], UR, down, left),
        (pack.at[pl.ds(112, 16)], UL, down, right),
    ]
    halo = [
        remote(src, part(slab, block), hs.at[n], hr.at[n], to_row, to_col)
        for n, (src, block, to_row, to_col) in enumerate(halo)
    ]
    for copy in halo:
        copy.start()

    chunks = []
    for k in range(9):
        chunk = 9 * col + k
        kind, place = chunk // 48, chunk % 48
        whole = place < 32
        to_chip = jnp.where(whole, place // 4, (place - 32) // 2)
        sub = jnp.where(whole, place % 4, 4 + place % 2)
        n = 6 * kind + sub
        to = 2 * to_chip + (n // 4) % 2
        src, dst = cw_hbm.at[pl.ds(32 * k, 32)], w.at[kind, sub]
        mine = n % 4 == low_row
        away = mine & (to != col)
        copy = remote(src, dst, ws.at[k], wr.at[n], row, to)
        chunks.append((away, copy))

        @pl.when(away)
        def _():
            copy.start()

        @pl.when(mine & (to == col))
        def _():
            pltpu.make_async_copy(src, dst, wr.at[n]).start()

    def slot(n):
        return w.at[n // 6, n % 6]

    def to_partner(n):
        return remote(slot(n), slot(n), wfs.at[n], wr.at[n], row, partner)

    def along_y(n):
        return [remote(slot(n), slot(n), wys.at[n, j], wr.at[n], ring[j], col) for j in range(3)]

    def first_here(n):
        return ((n // 4) % 2 == core) & (n % 4 == low_row)

    def wait_part(n):
        place = (4 * chip + n % 6) if n % 6 < 4 else (28 + 2 * chip + n % 6)
        source = (48 * (n // 6) + place) // 9

        @pl.when(source != col)
        def _():
            to_partner(n).wait_recv()

        @pl.when(source == col)
        def _():
            pltpu.make_async_copy(cw_hbm.at[pl.ds(0, 32)], slot(n), wr.at[n]).wait()

    cot_copies = [
        remote(cotp.at[(chip + d) % chips], gt.at[d], cs.at[d], cr.at[d], row, 2 * ((chip + d) % chips) + core)
        for d in range(1, chips)
    ]
    for copy in cot_copies:
        copy.start()
    gt[0] = cotp[chip]

    def window_all():
        slab[0:OWN, :] = fine[:, 768:2304]
        window = window_bias(
            jnp.where(row > 0, 1, 0), jnp.where(row < rows - 1, 1, 0),
            jnp.where(col > 0, 1, 0), jnp.where(col < cols - 1, 1, 0),
        )
        bias[:, 0:128] = window
        bias[:, 128:256] = window

    phase("window", window_all)

    def both_heads(block):
        return jnp.concatenate([block * even, block * odd], 0)

    def own_lanes(two):
        return jnp.where(lanes < 64, two[0:128], two[128:256])

    for copy in halo:
        copy.wait_recv()

    def fine_forward():
        for p in range(6):
            at = 128 * p
            query = both_heads(fine[:, at : at + 128] * SCALE)
            scores = dot_nt(slab[:, at : at + 128], query) + bias[...]
            weights = softmax_rows(scores).astype(BF)
            probs[p] = weights
            out = dot_tn(weights, slab[:, 768 + at : 768 + at + 128])
            att[:, at : at + 128] = own_lanes(out).astype(BF)
        i, t = iotas((128, 128))
        xm[...] = dot(pick(merge_token(i), t), att[...]).astype(BF)

    phase("fine_forward", fine_forward)
    for n in range(18):

        @pl.when(first_here(n))
        def _():
            wait_part(n)
            for copy in along_y(n):
                copy.start()
            to_partner(n).start()

    load.wait()

    def normalise(d):
        wide = jnp.concatenate([nb[0, d], nb[1, d]], 1).astype(F32)
        inverse = lax.rsqrt(jnp.mean(wide * wide, -1, keepdims=True) + 1e-06)
        normed[32 * d : 32 * d + 32, :] = (wide * inverse * gain).astype(BF)

    gather = []
    for half in range(2):

        def merge():
            def merge_step(n, _):
                at = pl.ds(pl.multiple_of(768 * half + 256 * n, 256), 256)
                total = dot(xm[0:32, :], mw[0:768, at])
                for s in range(1, 4):
                    total = total + dot(xm[32 * s : 32 * s + 32, :], mw[768 * s : 768 * s + 768, at])
                nb[half, 0, :, pl.ds(pl.multiple_of(256 * n, 256), 256)] = total.astype(BF)
                return 0

            lax.fori_loop(0, 3, merge_step, 0)

        phase("merge", merge)
        copies = [
            remote(
                nb.at[half, 0], nb.at[half, d], as_.at[half, d], ar.at[half, d],
                row, 2 * ((chip + d) % chips) + core,
            )
            for d in range(1, chips)
        ]
        for copy in copies:
            copy.start()
        gather.append(copies)
    normalise(0)

    for n in range(18):

        @pl.when(((n // 4) % 2 == core) & (n % 4 != low_row))
        def _():
            to_partner(n).wait_recv()
            to_partner(n).start()

    for d in range(1, chips):
        gather[0][d - 1].wait_recv()
        gather[1][d - 1].wait_recv()
        normalise(d)
    for n in range(18):

        @pl.when((n // 4) % 2 != core)
        def _():
            to_partner(n).wait_recv()

    def project(kind):
        return dot_nt(normed[...], w[kind].reshape(256, 1536)).astype(BF)

    def project_keys():
        kslab[0:tokens, :] = project(1)

    def project_values():
        vslab[0:tokens, :] = project(2)

    def project_query():
        qbuf[...] = project(0)

    phase("project_k", project_keys)
    swap_k = remote(kslab.at[pl.ds(0, tokens)], kslab.at[pl.ds(tokens, tokens)], ks.at[0], kr.at[0], row, partner)
    swap_k.start()
    phase("project_v", project_values)
    swap_v = remote(vslab.at[pl.ds(0, tokens)], vslab.at[pl.ds(tokens, tokens)], ks.at[1], kr.at[1], row, partner)
    swap_v.start()
    phase("project_q", project_query)
    for copy in cot_copies:
        copy.wait_recv()
    swap_k.wait_recv()
    swap_v.wait_recv()
    wide_lane = lax.broadcasted_iota(jnp.int32, (tokens, 128), 1)

    def head_refs(head):
        at = 128 * (head // 2)
        mask = (even, odd, even)[head]
        query = qbuf[:, at : at + 128] * mask * SCALE
        grad = gt[:, :, at : at + 128].reshape(tokens, 128) * mask
        return query, grad, kslab[:, at : at + 128], vslab[:, at : at + 128]

    def key_grads(low):
        span = slice(low, low + tokens)
        dks, dvs = [], []
        for head in range(3):
            query, grad, _, _ = head_refs(head)
            dks.append(dot(dsbuf[head, span, :], query))
            dvs.append(dot(pbuf[head, span, :], grad))
        return [jnp.concatenate([d[0] + d[1], d[2]], 1) for d in (dks, dvs)]

    def band():
        for head in range(3):
            query, grad, keys, values = head_refs(head)
            weights = softmax_rows(dot_nt(keys, query))
            pbuf[head] = weights.astype(BF)
            dp = dot_nt(values, grad)
            delta = jnp.sum(weights * dp, 0, keepdims=True)
            dsbuf[head] = (weights * (dp - delta)).astype(BF)
        for which, both in enumerate(key_grads(tokens)):
            dsend[which] = both.astype(BF)

    phase("band", band)
    swap_d = remote(dsend, drecv, ds_, dr_, row, partner)
    swap_d.start()

    def band_rest():
        outs, dqs = [], []
        for head in range(3):
            _, _, keys, values = head_refs(head)
            dqs.append(dot_tn(dsbuf[head], keys) * SCALE)
            outs.append(dot_tn(pbuf[head], values))
        dqkv[:, 0:128] = jnp.where(wide_lane < 64, dqs[0], dqs[1]).astype(BF)
        dqkv[:, 128:256] = dqs[2].astype(BF)
        out = jnp.concatenate([jnp.where(wide_lane < 64, outs[0], outs[1]), outs[2]], 1)
        osend[...] = out.astype(BF).reshape(chips, 32, 256)
        corecv[chip] = osend[0]

    phase("band_rest", band_rest)
    out_copies = [
        remote(osend.at[d], corecv.at[chip], os_.at[d], orr.at[d], row, 2 * ((chip + chips - d) % chips) + core)
        for d in range(1, chips)
    ]
    own_grads = key_grads(0)
    swap_d.wait_recv()
    for which in range(2):
        at = 256 + 256 * which
        dqkv[:, at : at + 256] = (own_grads[which] + drecv[which].astype(F32)).astype(BF)

    scatter = []
    for half in (1, 0):
        first = half * (chips // 2)
        span = slice(first * 32, first * 32 + tokens // 2)

        def back_project():
            def back_step(n, _):
                at = pl.ds(pl.multiple_of(256 * n, 256), 256)
                total = dot(dqkv[span, 0:256], w[0, :, :, at].reshape(256, 256))
                for kind in range(1, 3):
                    grad = dqkv[span, 256 * kind : 256 * kind + 256]
                    total = total + dot(grad, w[kind, :, :, at].reshape(256, 256))
                ngs[first : first + chips // 2, :, at] = total.astype(BF).reshape(chips // 2, 32, 256)
                return 0

            lax.fori_loop(0, 6, back_step, 0)

        phase("back_project", back_project)
        copies = [
            remote(ngs.at[d], rs.at[d], rss.at[d], rsr.at[d], row, 2 * ((chip + chips - d) % chips) + core)
            for d in range(max(first, 1), first + chips // 2)
        ]
        for copy in copies:
            copy.start()
        scatter += copies
    for copy in out_copies:
        copy.start()
    for copy in scatter:
        copy.wait_recv()

    def unmerge():
        total = ngs[0].astype(F32)
        for d in range(1, chips):
            total = total + rs[d].astype(F32)
        wide = jnp.concatenate([nb[0, 0], nb[1, 0]], 1).astype(F32)
        inverse = lax.rsqrt(jnp.mean(wide * wide, -1, keepdims=True) + 1e-06)
        scaled = total * gain
        cgrad = inverse * (scaled - wide * (inverse * inverse * jnp.mean(scaled * wide, -1, keepdims=True)))
        cgrad = cgrad.astype(BF)

        def unmerge_step(n, _):
            at = pl.ds(pl.multiple_of(256 * n, 256), 256)
            mg[at, :] = dot_nt(mw[at, :], cgrad).astype(BF)
            return 0

        lax.fori_loop(0, 12, unmerge_step, 0)
        token, t = iotas((128, 32))
        total = jnp.zeros((128, 768), F32)
        for s in range(4):
            total = total + dot_nt(pick(merge_token(32 * s + t), token), mg[768 * s : 768 * s + 768, :])
        ag[...] = total.astype(BF)

    phase("unmerge", unmerge)

    def fine_backward_halo():
        for p in range(6):
            at = 128 * p
            query = both_heads(fine[:, at : at + 128] * SCALE)
            grad = both_heads(ag[:, at : at + 128])
            weights_low = probs[p]
            weights = weights_low.astype(F32)
            dp = dot_nt(slab[:, 768 + at : 768 + at + 128], grad)
            delta = jnp.sum(weights * dp, 0, keepdims=True)
            ds_low = (weights * (dp - delta)).astype(BF)
            dscore[p] = ds_low
            gsend[:, at : at + 128] = dot(ds_low[OWN:], query).astype(BF)
            gsend[:, 768 + at : 768 + at + 128] = dot(weights_low[OWN:], grad).astype(BF)

    phase("fine_back_halo", fine_backward_halo)
    back = [
        (UP, 48, up, col), (DOWN, 0, down, col), (LEFT, 128, row, left), (RIGHT, 96, row, right),
        (UL, 208, up, left), (UR, 192, up, right), (DL, 176, down, left), (DR, 160, down, right),
    ]
    back = [
        remote(
            gsend.at[pl.ds(block[0] - OWN, block[1])], gr.at[pl.ds(to, block[1])],
            gs.at[n], grs.at[n], to_row, to_col,
        )
        for n, (block, to, to_row, to_col) in enumerate(back)
    ]
    for copy in back:
        copy.start()

    def fine_backward_own():
        for p in range(6):
            at = 128 * p
            query = both_heads(fine[:, at : at + 128] * SCALE)
            grad = both_heads(ag[:, at : at + 128])
            gown[:, at : at + 128] = dot(dscore[p, 0:OWN, :], query)
            gown[:, 768 + at : 768 + at + 128] = dot(probs[p, 0:OWN, :], grad)
            dq = dot_tn(dscore[p], slab[:, at : at + 128]) * SCALE
            fg_out[:, at : at + 128] = own_lanes(dq).astype(BF)

    phase("fine_back_own", fine_backward_own)

    for d in range(1, chips):
        source = (chip + d) % chips
        remote(osend.at[d], corecv.at[source], os_.at[d], orr.at[d], row, 2 * source + core).wait_recv()

    def coarse_output():
        for c in range(chips):
            co_out[:, 128 * c : 128 * c + 128] = corecv[c, :, 0:128]
        for c in range(0, chips, 2):
            at = 1024 + 64 * c
            co_out[:, at : at + 128] = jnp.concatenate([corecv[c, :, 128:192], corecv[c + 1, :, 128:192]], 1)

    phase("coarse_output", coarse_output)
    for copy in back:
        copy.wait_recv()

    def finish():
        i, t = iotas((128, 128))
        kv_grad = gown[...] + dot(pick(pack_token(t), i), gr[96:224, :])
        fg_out[48:80, 768:2304] = kv_grad[48:80].astype(BF)
        fg_out[0:48, 768:2304] = (kv_grad[0:48] + gr[0:48, :].astype(F32)).astype(BF)
        fg_out[80:128, 768:2304] = (kv_grad[80:128] + gr[48:96, :].astype(F32)).astype(BF)

    phase("finish", finish)
    for copy in halo + cot_copies + gather[0] + gather[1] + [swap_k, swap_v, swap_d] + out_copies + scatter + back:
        copy.wait_send()
    for away, copy in chunks:

        @pl.when(away)
        def _():
            copy.wait_send()

    for n in range(18):

        @pl.when((n // 4) % 2 == core)
        def _():
            to_partner(n).wait_send()

        @pl.when(first_here(n))
        def _():
            for copy in along_y(n):
                copy.wait_send()


def carry(a, b, a_out, b_out):
    a_out[...] = a[...]
    b_out[...] = b[...]


def shards(mesh_rows, mesh_cols, fine_qkv, merge_weight, coarse_weight, norm_gain, cotangent):
    chips = mesh_cols // 2
    tokens = 32 * chips
    vmem = pl.BlockSpec(memory_space=pltpu.VMEM)
    hbm = pl.BlockSpec(memory_space=pl.ANY)
    dma = pltpu.SemaphoreType.DMA

    def low(*shape):
        return pltpu.VMEM(shape, BF)

    def full(*shape):
        return pltpu.VMEM(shape, F32)

    coarse_out, fine_grad = pl.pallas_call(
        functools.partial(kernel, mesh_rows, mesh_cols),
        out_shape=(jax.ShapeDtypeStruct((32, 1536), BF), jax.ShapeDtypeStruct((128, 2304), BF)),
        in_specs=[hbm] * 5,
        out_specs=(vmem, vmem),
        scratch_shapes=[
            low(128, 2304), low(32, 1536), full(1536), low(3072, 1536), low(SLAB, 1536), low(128, 1536), full(SLAB, 256),
            low(6, SLAB, 256), low(6, SLAB, 256), low(128, 768), low(128, 768),
            low(3, 8, 32, 1536), low(2, chips, 32, 768), low(tokens, 1536),
            low(chips, 32, 256), low(chips, 32, 256), low(tokens, 256), low(2 * tokens, 256),
            low(2 * tokens, 256), low(3, 2 * tokens, tokens), low(3, 2 * tokens, tokens), low(2, tokens, 256), low(2, tokens, 256), low(tokens, 768),
            low(chips, 32, 256), low(chips, 32, 256),
            low(chips, 32, 1536), low(chips, 32, 1536), low(3072, 32), low(128, 768), full(128, 1536),
            low(224, 1536), low(224, 1536),
            dma, dma, dma, dma, dma((8,)), dma((8,)), dma((8,)), dma((8,)), dma((9,)), dma((18,)),
            dma((18, 3)), dma((18,)), dma((2, chips)), dma((2, chips)), dma((chips,)), dma((chips,)),
            dma((2,)), dma((2,)), dma, dma, dma((chips,)), dma((chips,)), dma((chips,)), dma((chips,)),
        ],
        compiler_params=pltpu.CompilerParams(
            collective_id=0, has_side_effects=True, vmem_limit_bytes=56 * 1024 * 1024
        ),
    )(
        fine_qkv.reshape(128, 2304),
        merge_weight,
        coarse_weight.T,
        norm_gain,
        cotangent.reshape(32, 1536),
    )
    coarse_out, fine_grad = pl.pallas_call(
        carry,
        out_shape=(jax.ShapeDtypeStruct((32, 1536), BF), jax.ShapeDtypeStruct((128, 2304), BF)),
        in_specs=[vmem, vmem],
        out_specs=(vmem, vmem),
    )(coarse_out, fine_grad)
    return coarse_out.reshape(4, 8, 1536), fine_grad.reshape(8, 16, 2304)


def solution(mesh):
    placed = (P("row", "col", None), P(), P(None, "col"), P(), P("row", "col", None))
    return jax.shard_map(
        functools.partial(shards, mesh.shape["row"], mesh.shape["col"]),
        mesh=mesh,
        in_specs=placed,
        out_specs=(P("row", "col", None), P("row", "col", None)),
        check_vma=False,
    )
```

```python
import functools

import jax
import jax.numpy as jnp
from jax import lax
from jax.experimental import pallas as pl
from jax.experimental.pallas import tpu as pltpu
from jax.sharding import PartitionSpec as P

MESH = pl.DeviceIdType.MESH
BF = jnp.bfloat16
F32 = jnp.float32
HD = 64
SCALE = HD ** (-0.5)
NEG = -1e30

OWN, SLAB = 128, 352
UP, DOWN, LEFT, RIGHT, UL, UR, DL, DR = (
    (128, 48), (176, 48), (224, 32), (256, 32), (288, 16), (304, 16), (320, 16), (336, 16),
)


def iotas(shape):
    return lax.broadcasted_iota(jnp.int32, shape, 0), lax.broadcasted_iota(jnp.int32, shape, 1)


def pick(index, other):
    return jnp.where(index == other, 1.0, 0.0).astype(BF)


def pack_token(i):
    j = i & 31
    strip_col = j >> 3
    strip = (j & 7) * 16 + strip_col + jnp.where(i >= 32, 13, 0)
    strip = jnp.where(strip_col < 3, strip, -1)
    j = i & 15
    k = (i - 64) >> 4
    col, row = j >> 2, j & 3
    corner = (row + jnp.where(k >= 2, 5, 0)) * 16 + col + (k & 1) * 13
    corner = jnp.where(jnp.maximum(row, col) < 3, corner, -1)
    return jnp.where(i < 64, strip, corner)


def merge_token(i):
    t, s = i & 31, i >> 5
    return (2 * (t >> 3) + (s >> 1)) * 16 + 2 * (t & 7) + (s & 1)


def window_bias(up_ok, down_ok, left_ok, right_ok):
    i, lane = iotas((SLAB, 128))
    query_row, query_col = lane >> 4, lane & 15
    far = 1000
    j = i - 128
    edge_row = (j >> 4) + jnp.where(i < 176, -3, 5)
    edge_row = jnp.where(jnp.where(i < 176, up_ok, down_ok) > 0, edge_row, far)
    j = (i - 224) & 31
    strip_col = j >> 3
    strip_ok = jnp.where(i < 256, left_ok, right_ok) * jnp.where(strip_col < 3, 1, 0)
    strip_row = jnp.where(strip_ok > 0, j & 7, far)
    strip_col = strip_col + jnp.where(i < 256, -3, 16)
    j, k = (i - 288) & 15, (i - 288) >> 4
    col, row = j >> 2, j & 3
    corner_ok = jnp.where(k < 2, up_ok, down_ok) * jnp.where((k & 1) == 0, left_ok, right_ok)
    corner_ok = corner_ok * jnp.where(jnp.maximum(row, col) < 3, 1, 0)
    corner_row = jnp.where(corner_ok > 0, row + jnp.where(k < 2, -3, 8), far)
    corner_col = col + jnp.where((k & 1) == 0, -3, 16)
    key_row = jnp.where(
        i < 128, i >> 4, jnp.where(i < 224, edge_row, jnp.where(i < 288, strip_row, corner_row))
    )
    key_col = jnp.where(i < 224, i & 15, jnp.where(i < 288, strip_col, corner_col))
    gap = jnp.maximum(jnp.abs(key_row - query_row), jnp.abs(key_col - query_col))
    return jnp.where(gap <= 3, 0.0, NEG)


def dot(a, b):
    return jnp.dot(a, b, preferred_element_type=F32)


def dot_nt(a, b):
    return lax.dot_general(a, b, (((1,), (1,)), ((), ())), preferred_element_type=F32)


def dot_tn(a, b):
    return lax.dot_general(a, b, (((0,), (0,)), ((), ())), preferred_element_type=F32)


def softmax_rows(scores):
    highest = jnp.max(scores, 0, keepdims=True)
    expd = jnp.exp(scores - highest)
    return expd * (1.0 / jnp.sum(expd, 0, keepdims=True))


def phase(name, work):
    work()


def kernel(
    rows, cols,
    fine_hbm, mw_hbm, cw_hbm, gain_hbm, cot_hbm,
    co_out, fg_out,
    fine, cot, gain_flat, mw, slab, pack, bias, hbias, probs, lse, attf, xm, qmsg, qpack, amsg, apack, qh, ah,
    w, nb, normed, cotp, gt, qbuf, kslab, vslab, pbuf, dsbuf, dsend, drecv, dqkv, osend, corecv,
    ngs, rs, mg, gown,
    fine_sem, cot_sem, gain_sem, mw_sem, hs, hr, qs, qr, gs, grs, ws, wr, wys, wfs, as_, ar, cs, cr, ks, kr, ds_, dr_, os_, orr, rss, rsr,
):
    row, col = lax.axis_index("row"), lax.axis_index("col")
    chip, core = col // 2, col % 2
    chips = cols // 2
    tokens = 32 * chips
    up, down = (row + rows - 1) % rows, (row + 1) % rows
    left, right = (col + cols - 1) % cols, (col + 1) % cols
    partner = col + 1 - 2 * core
    high, low_row = row // 4, row % 4
    ring = [4 * high + (low_row + j) % 4 for j in range(1, 4)]

    def remote(src, dst, send, recv, to_row, to_col):
        return pltpu.make_async_remote_copy(
            src_ref=src, dst_ref=dst, send_sem=send, recv_sem=recv,
            device_id=(to_row, to_col), device_id_type=MESH,
        )

    def part(ref, block):
        return ref.at[pl.ds(block[0], block[1])]

    barrier = pltpu.get_barrier_semaphore()
    for step in range(1, cols):
        pl.semaphore_signal(barrier, inc=1, device_id=(row, (col + step) % cols), device_id_type=MESH)
    for to_row in (up, down):
        for to_col in (left, col, right):
            pl.semaphore_signal(barrier, inc=1, device_id=(to_row, to_col), device_id_type=MESH)
    for to_row in ring:
        pl.semaphore_signal(barrier, inc=1, device_id=(to_row, col), device_id_type=MESH)

    load_fine = pltpu.make_async_copy(fine_hbm, fine, fine_sem)
    load_fine.start()
    load_cot = pltpu.make_async_copy(cot_hbm, cot, cot_sem)
    load_cot.start()
    load_gain = pltpu.make_async_copy(gain_hbm, gain_flat, gain_sem)
    load_gain.start()
    load = pltpu.make_async_copy(mw_hbm, mw, mw_sem)
    load.start()

    lane = lax.broadcasted_iota(jnp.int32, (1, 128), 1)
    even = jnp.where(lane < 64, 1.0, 0.0).astype(BF)
    odd = jnp.where(lane < 64, 0.0, 1.0).astype(BF)
    _, lanes = iotas((128, 128))

    def pack_all():
        i, t = iotas((128, 128))
        pack[...] = dot(pick(pack_token(i), t), fine[:, 768:2304]).astype(BF)
        for c in range(chips):
            cotp[c, :, 0:128] = cot[:, 128 * c : 128 * c + 128]
            at = 1024 + 64 * c
            cotp[c, :, 128:256] = jnp.concatenate([cot[:, at : at + 64], jnp.zeros((32, 64), BF)], 1)
        for kind in range(3):
            w[kind, 6:8] = jnp.zeros((2, 32, 1536), BF)

    load_fine.wait()
    load_cot.wait()
    load_gain.wait()
    gain = gain_flat[...].reshape(1, 1536)
    phase("pack", pack_all)

    pl.semaphore_wait(barrier, cols + 8)

    def to_neighbours(rows_of, packed, into, send, recv):
        routes = [
            (rows_of(0), DOWN, up, col),
            (rows_of(80), UP, down, col),
            (packed.at[pl.ds(0, 32)], RIGHT, row, left),
            (packed.at[pl.ds(32, 32)], LEFT, row, right),
            (packed.at[pl.ds(64, 16)], DR, up, left),
            (packed.at[pl.ds(80, 16)], DL, up, right),
            (packed.at[pl.ds(96, 16)], UR, down, left),
            (packed.at[pl.ds(112, 16)], UL, down, right),
        ]
        return [
            remote(src, into(block), send.at[n], recv.at[n], to_row, to_col)
            for n, (src, block, to_row, to_col) in enumerate(routes)
        ]

    def halo_rows(ref):
        return lambda block: ref.at[pl.ds(block[0] - OWN, block[1])]

    halo = to_neighbours(
        lambda at: fine.at[pl.ds(at, 48), pl.ds(768, 1536)], pack, lambda block: part(slab, block), hs, hr
    )
    for copy in halo:
        copy.start()

    chunks = []
    for k in range(9):
        chunk = 9 * col + k
        kind, place = chunk // 48, chunk % 48
        whole = place < 32
        to_chip = jnp.where(whole, place // 4, (place - 32) // 2)
        sub = jnp.where(whole, place % 4, 4 + place % 2)
        n = 6 * kind + sub
        to = 2 * to_chip + (n // 4) % 2
        src, dst = cw_hbm.at[pl.ds(32 * k, 32)], w.at[kind, sub]
        mine = n % 4 == low_row
        away = mine & (to != col)
        copy = remote(src, dst, ws.at[k], wr.at[n], row, to)
        chunks.append((away, copy))

        @pl.when(away)
        def _():
            copy.start()

        @pl.when(mine & (to == col))
        def _():
            pltpu.make_async_copy(src, dst, wr.at[n]).start()

    def slot(n):
        return w.at[n // 6, n % 6]

    def to_partner(n):
        return remote(slot(n), slot(n), wfs.at[n], wr.at[n], row, partner)

    def along_y(n):
        return [remote(slot(n), slot(n), wys.at[n, j], wr.at[n], ring[j], col) for j in range(3)]

    def each_part(of_core, places, work):
        for i in range(3):
            for place in places:
                n = 4 * (of_core + 2 * i) + place
                if i < 2:
                    work(n)
                else:

                    @pl.when(n < 18)
                    def _():
                        work(n)

    def wait_part(n):
        place = jnp.where(n % 6 < 4, 4 * chip + n % 6, 28 + 2 * chip + n % 6)
        source = (48 * (n // 6) + place) // 9

        @pl.when(source != col)
        def _():
            to_partner(n).wait_recv()

        @pl.when(source == col)
        def _():
            pltpu.make_async_copy(cw_hbm.at[pl.ds(0, 32)], slot(n), wr.at[n]).wait()

    cot_copies = [
        remote(cotp.at[(chip + d) % chips], gt.at[d], cs.at[d], cr.at[d], row, 2 * ((chip + d) % chips) + core)
        for d in range(1, chips)
    ]
    gt[0] = cotp[chip]

    def window_all():
        slab[0:OWN, :] = fine[:, 768:2304]
        window = window_bias(
            jnp.where(row > 0, 1, 0), jnp.where(row < rows - 1, 1, 0),
            jnp.where(col > 0, 1, 0), jnp.where(col < cols - 1, 1, 0),
        )
        bias[:, 0:128] = window
        bias[:, 128:256] = window
        outer = jnp.concatenate([window[OWN:SLAB], jnp.full((32, 128), NEG, F32)], 0).T
        hbias[:, 0:256] = outer
        hbias[:, 256:512] = outer
        for ref in (qh, ah):
            ref[224:256, :] = jnp.zeros((32, 896), BF)

    phase("window", window_all)

    def both_heads(block):
        return jnp.concatenate([block * even, block * odd], 0)

    def own_lanes(two):
        return jnp.where(lanes < 64, two[0:128], two[128:256])

    for copy in halo:
        copy.wait_recv()

    for copy in cot_copies:
        copy.start()

    def fine_forward():
        lse[12:16, :] = jnp.zeros((4, 128), F32)
        outs = []
        for p in range(6):
            at = 128 * p
            query = both_heads(fine[:, at : at + 128] * SCALE)
            scores = dot_nt(slab[:, at : at + 128], query) + bias[...]
            highest = jnp.max(scores, 0, keepdims=True)
            expd = jnp.exp(scores - highest)
            total = jnp.sum(expd, 0, keepdims=True)
            weights = (expd * (1.0 / total)).astype(BF)
            probs[p] = weights
            norm = highest + jnp.log(total)
            lse[2 * p : 2 * p + 1, :] = norm[:, 0:128]
            lse[2 * p + 1 : 2 * p + 2, :] = norm[:, 128:256]
            out = own_lanes(dot_tn(weights, slab[:, 768 + at : 768 + at + 128]))
            attf[:, at : at + 128] = out
            outs.append(out.astype(BF))
        i, t = iotas((128, 128))
        xm[...] = dot(pick(merge_token(i), t), jnp.concatenate(outs, 1)).astype(BF)

    phase("fine_forward", fine_forward)
    def pass_on(n):
        wait_part(n)
        for copy in along_y(n):
            copy.start()
        to_partner(n).start()

    each_part(core, [low_row], pass_on)
    load.wait()

    def normalise(d):
        wide = jnp.concatenate([nb[0, d], nb[1, d]], 1).astype(F32)
        inverse = lax.rsqrt(jnp.mean(wide * wide, -1, keepdims=True) + 1e-06)
        normed[32 * d : 32 * d + 32, :] = (wide * inverse * gain).astype(BF)

    gather = []
    for half in range(2):

        def merge():
            at = slice(768 * half, 768 * half + 768)
            total = dot(xm[0:32, :], mw[0:768, at])
            for s in range(1, 4):
                total = total + dot(xm[32 * s : 32 * s + 32, :], mw[768 * s : 768 * s + 768, at])
            nb[half, 0] = total.astype(BF)

        phase("merge", merge)
        copies = [
            remote(
                nb.at[half, 0], nb.at[half, d], as_.at[half, d], ar.at[half, d],
                row, 2 * ((chip + d) % chips) + core,
            )
            for d in range(1, chips)
        ]
        for copy in copies:
            copy.start()
        gather.append(copies)
    normalise(0)

    def query_message():
        norm = lse[...]
        high = norm.astype(BF).astype(F32)
        middle = (norm - high).astype(BF).astype(F32)
        terms = [high, middle, norm - high - middle, jnp.zeros((80, 128), F32)]
        qmsg[:, 0:768] = fine[:, 0:768]
        qmsg[:, 768:896] = jnp.concatenate(terms, 0).T.astype(BF)
        i, t = iotas((128, 128))
        qpack[...] = dot(pick(pack_token(i), t), qmsg[...]).astype(BF)

    phase("query_message", query_message)
    def pass_over(n):
        to_partner(n).wait_recv()
        to_partner(n).start()

    each_part(core, [(low_row + j) % 4 for j in range(1, 4)], pass_over)

    for d in range(1, chips):
        gather[0][d - 1].wait_recv()
        gather[1][d - 1].wait_recv()
        normalise(d)
    each_part(1 - core, range(4), lambda n: to_partner(n).wait_recv())

    def project(kind):
        return dot_nt(normed[...], w[kind].reshape(256, 1536)).astype(BF)

    def project_keys():
        kslab[0:tokens, :] = project(1)

    def project_values():
        vslab[0:tokens, :] = project(2)

    def project_query():
        qbuf[...] = project(0)

    phase("project_k", project_keys)
    swap_k = remote(kslab.at[pl.ds(0, tokens)], kslab.at[pl.ds(tokens, tokens)], ks.at[0], kr.at[0], row, partner)
    swap_k.start()
    phase("project_v", project_values)
    swap_v = remote(vslab.at[pl.ds(0, tokens)], vslab.at[pl.ds(tokens, tokens)], ks.at[1], kr.at[1], row, partner)
    swap_v.start()
    rim_queries = to_neighbours(lambda at: qmsg.at[pl.ds(at, 48)], qpack, halo_rows(qh), qs, qr)
    for copy in rim_queries:
        copy.start()
    phase("project_q", project_query)
    for copy in cot_copies:
        copy.wait_recv()
    swap_k.wait_recv()
    swap_v.wait_recv()
    wide_lane = lax.broadcasted_iota(jnp.int32, (tokens, 128), 1)

    def head_refs(head):
        at = 128 * (head // 2)
        mask = (even, odd, even)[head]
        query = qbuf[:, at : at + 128] * mask * SCALE
        grad = gt[:, :, at : at + 128].reshape(tokens, 128) * mask
        return query, grad, kslab[:, at : at + 128], vslab[:, at : at + 128]

    def key_grads(low):
        span = slice(low, low + tokens)
        dks, dvs = [], []
        for head in range(3):
            query, grad, _, _ = head_refs(head)
            dks.append(dot(dsbuf[head, span, :], query))
            dvs.append(dot(pbuf[head, span, :], grad))
        return [jnp.concatenate([d[0] + d[1], d[2]], 1) for d in (dks, dvs)]

    def band():
        for head in range(3):
            query, grad, keys, values = head_refs(head)
            weights = softmax_rows(dot_nt(keys, query))
            pbuf[head] = weights.astype(BF)
            dp = dot_nt(values, grad)
            delta = jnp.sum(weights * dp, 0, keepdims=True)
            dsbuf[head] = (weights * (dp - delta)).astype(BF)
        for which, both in enumerate(key_grads(tokens)):
            dsend[which] = both.astype(BF)

    phase("band", band)
    swap_d = remote(dsend, drecv, ds_, dr_, row, partner)
    swap_d.start()

    def band_rest():
        outs, dqs = [], []
        for head in range(3):
            _, _, keys, values = head_refs(head)
            dqs.append(dot_tn(dsbuf[head], keys) * SCALE)
            outs.append(dot_tn(pbuf[head], values))
        dqkv[:, 0:128] = jnp.where(wide_lane < 64, dqs[0], dqs[1]).astype(BF)
        dqkv[:, 128:256] = dqs[2].astype(BF)
        out = jnp.concatenate([jnp.where(wide_lane < 64, outs[0], outs[1]), outs[2]], 1)
        osend[...] = out.astype(BF).reshape(chips, 32, 256)
        corecv[chip] = osend[0]

    phase("band_rest", band_rest)
    out_copies = [
        remote(osend.at[d], corecv.at[chip], os_.at[d], orr.at[d], row, 2 * ((chip + chips - d) % chips) + core)
        for d in range(1, chips)
    ]
    own_grads = key_grads(0)
    swap_d.wait_recv()
    for which in range(2):
        at = 256 + 256 * which
        dqkv[:, at : at + 256] = (own_grads[which] + drecv[which].astype(F32)).astype(BF)

    scatter = []
    for half in (1, 0):
        first = half * (chips // 2)
        span = slice(first * 32, first * 32 + tokens // 2)

        def back_project():
            for n in range(3):
                at = slice(512 * n, 512 * n + 512)
                total = dot(dqkv[span, :], w[:, :, :, at].reshape(768, 512))
                ngs[first : first + chips // 2, :, at] = total.astype(BF).reshape(chips // 2, 32, 512)

        phase("back_project", back_project)
        copies = [
            remote(ngs.at[d], rs.at[d], rss.at[d], rsr.at[d], row, 2 * ((chip + chips - d) % chips) + core)
            for d in range(max(first, 1), first + chips // 2)
        ]
        for copy in copies:
            copy.start()
        scatter += copies
    for copy in scatter:
        copy.wait_recv()

    def unmerge():
        total = ngs[0].astype(F32)
        for d in range(1, chips):
            total = total + rs[d].astype(F32)
        wide = jnp.concatenate([nb[0, 0], nb[1, 0]], 1).astype(F32)
        inverse = lax.rsqrt(jnp.mean(wide * wide, -1, keepdims=True) + 1e-06)
        scaled = total * gain
        cgrad = inverse * (scaled - wide * (inverse * inverse * jnp.mean(scaled * wide, -1, keepdims=True)))
        cgrad = cgrad.astype(BF)

        for n in range(3):
            at = slice(1024 * n, 1024 * n + 1024)
            mg[at, :] = dot_nt(mw[at, :], cgrad).astype(BF)
        token, t = iotas((128, 32))
        total = jnp.zeros((128, 768), F32)
        for s in range(4):
            total = total + dot_nt(pick(merge_token(32 * s + t), token), mg[768 * s : 768 * s + 768, :])
        amsg[:, 0:768] = total.astype(BF)
        product = amsg[:, 0:768].astype(F32) * attf[...]
        feature, lane_of = iotas((768, 128))
        heads = jnp.where(lane_of < 32, pick(feature >> 6, lane_of & 15).astype(F32), 0.0).astype(BF)
        high = product.astype(BF)
        delta = dot(high, heads) + dot((product - high.astype(F32)).astype(BF), heads)
        high = delta.astype(BF).astype(F32)
        amsg[:, 768:896] = jnp.where(lanes < 16, high, delta - high).astype(BF)
        i, t = iotas((128, 128))
        apack[...] = dot(pick(pack_token(i), t), amsg[...]).astype(BF)

    phase("unmerge", unmerge)

    rim_grads = to_neighbours(lambda at: amsg.at[pl.ds(at, 48)], apack, halo_rows(ah), gs, grs)
    for copy in rim_grads:
        copy.start()
    for copy in out_copies:
        copy.start()

    def fine_backward_own():
        for p in range(6):
            at = 128 * p
            query = both_heads(fine[:, at : at + 128] * SCALE)
            grad = both_heads(amsg[:, at : at + 128])
            weights_low = probs[p]
            weights = weights_low.astype(F32)
            dp = dot_nt(slab[:, 768 + at : 768 + at + 128], grad)
            delta = jnp.sum(weights * dp, 0, keepdims=True)
            ds_low = (weights * (dp - delta)).astype(BF)
            gown[:, at : at + 128] = dot(ds_low[0:OWN], query)
            gown[:, 768 + at : 768 + at + 128] = dot(weights_low[0:OWN], grad)
            dq = dot_tn(ds_low, slab[:, at : at + 128]) * SCALE
            fg_out[:, at : at + 128] = own_lanes(dq).astype(BF)

    phase("fine_back_own", fine_backward_own)

    for copy in rim_queries:
        copy.wait_recv()
    terms = qh[:, 768:896].astype(F32).T
    rim_lse = terms[0:16] + terms[16:32] + terms[32:48]
    for copy in rim_grads:
        copy.wait_recv()

    def fine_backward_rim():
        terms = ah[:, 768:896].astype(F32).T
        rim_delta = terms[0:16] + terms[16:32]

        def row_of(stat, p):
            return jnp.concatenate([stat[2 * p : 2 * p + 1], stat[2 * p + 1 : 2 * p + 2]], 1)

        for p in range(6):
            at, val = 128 * p, 768 + 128 * p
            query = both_heads(qh[:, at : at + 128] * SCALE)
            grad = both_heads(ah[:, at : at + 128])
            scores = dot_nt(slab[0:OWN, at : at + 128], query) + hbias[...]
            weights = jnp.exp(scores - row_of(rim_lse, p))
            dp = dot_nt(slab[0:OWN, val : val + 128], grad)
            ds_low = (weights * (dp - row_of(rim_delta, p))).astype(BF)
            dk = gown[:, at : at + 128] + dot(ds_low, query)
            dv = gown[:, val : val + 128] + dot(weights.astype(BF), grad)
            fg_out[:, 768 + at : 896 + at] = dk.astype(BF)
            fg_out[:, 768 + val : 896 + val] = dv.astype(BF)

    phase("fine_back_rim", fine_backward_rim)
    for d in range(1, chips):
        source = (chip + d) % chips
        remote(osend.at[d], corecv.at[source], os_.at[d], orr.at[d], row, 2 * source + core).wait_recv()

    def coarse_output():
        for c in range(chips):
            co_out[:, 128 * c : 128 * c + 128] = corecv[c, :, 0:128]
        for c in range(0, chips, 2):
            at = 1024 + 64 * c
            co_out[:, at : at + 128] = jnp.concatenate([corecv[c, :, 128:192], corecv[c + 1, :, 128:192]], 1)

    phase("coarse_output", coarse_output)
    for copy in halo + cot_copies + gather[0] + gather[1] + [swap_k, swap_v, swap_d] + out_copies + scatter + rim_queries + rim_grads:
        copy.wait_send()
    for away, copy in chunks:

        @pl.when(away)
        def _():
            copy.wait_send()

    def sent_along_y(n):
        for copy in along_y(n):
            copy.wait_send()

    each_part(core, range(4), lambda n: to_partner(n).wait_send())
    each_part(core, [low_row], sent_along_y)


def carry(a, b, a_out, b_out):
    a_out[...] = a[...]
    b_out[...] = b[...]


def shards(mesh_rows, mesh_cols, fine_qkv, merge_weight, coarse_weight, norm_gain, cotangent):
    chips = mesh_cols // 2
    tokens = 32 * chips
    vmem = pl.BlockSpec(memory_space=pltpu.VMEM)
    hbm = pl.BlockSpec(memory_space=pl.ANY)
    dma = pltpu.SemaphoreType.DMA

    def low(*shape):
        return pltpu.VMEM(shape, BF)

    def full(*shape):
        return pltpu.VMEM(shape, F32)

    coarse_out, fine_grad = pl.pallas_call(
        functools.partial(kernel, mesh_rows, mesh_cols),
        out_shape=(jax.ShapeDtypeStruct((32, 1536), BF), jax.ShapeDtypeStruct((128, 2304), BF)),
        in_specs=[hbm] * 5,
        out_specs=(vmem, vmem),
        scratch_shapes=[
            low(128, 2304), low(32, 1536), full(1536), low(3072, 1536), low(SLAB, 1536), low(128, 1536), full(SLAB, 256),
            full(128, 512), low(6, SLAB, 256),
            full(16, 128), full(128, 768), low(128, 768),
            low(128, 896), low(128, 896), low(128, 896), low(128, 896), low(256, 896), low(256, 896),
            low(3, 8, 32, 1536), low(2, chips, 32, 768), low(tokens, 1536),
            low(chips, 32, 256), low(chips, 32, 256), low(tokens, 256), low(2 * tokens, 256),
            low(2 * tokens, 256), low(3, 2 * tokens, tokens), low(3, 2 * tokens, tokens), low(2, tokens, 256), low(2, tokens, 256), low(tokens, 768),
            low(chips, 32, 256), low(chips, 32, 256),
            low(chips, 32, 1536), low(chips, 32, 1536), low(3072, 32), full(128, 1536),
            dma, dma, dma, dma, dma((8,)), dma((8,)), dma((8,)), dma((8,)), dma((8,)), dma((8,)), dma((9,)), dma((18,)),
            dma((18, 3)), dma((18,)), dma((2, chips)), dma((2, chips)), dma((chips,)), dma((chips,)),
            dma((2,)), dma((2,)), dma, dma, dma((chips,)), dma((chips,)), dma((chips,)), dma((chips,)),
        ],
        compiler_params=pltpu.CompilerParams(
            collective_id=0, has_side_effects=True, vmem_limit_bytes=56 * 1024 * 1024
        ),
    )(
        fine_qkv.reshape(128, 2304),
        merge_weight,
        coarse_weight.T,
        norm_gain,
        cotangent.reshape(32, 1536),
    )
    coarse_out, fine_grad = pl.pallas_call(
        carry,
        out_shape=(jax.ShapeDtypeStruct((32, 1536), BF), jax.ShapeDtypeStruct((128, 2304), BF)),
        in_specs=[vmem, vmem],
        out_specs=(vmem, vmem),
    )(coarse_out, fine_grad)
    return coarse_out.reshape(4, 8, 1536), fine_grad.reshape(8, 16, 2304)


def solution(mesh):
    placed = (P("row", "col", None), P(), P(None, "col"), P(), P("row", "col", None))
    return jax.shard_map(
        functools.partial(shards, mesh.shape["row"], mesh.shape["col"]),
        mesh=mesh,
        in_specs=placed,
        out_specs=(P("row", "col", None), P("row", "col", None)),
        check_vma=False,
    )
```

```python
import functools

import jax
import jax.numpy as jnp
from jax import lax
from jax.experimental import pallas as pl
from jax.experimental.pallas import tpu as pltpu
from jax.sharding import PartitionSpec as P

MESH = pl.DeviceIdType.MESH
BF = jnp.bfloat16
F32 = jnp.float32
HD = 64
SCALE = HD ** (-0.5)
NEG = -1e30

OWN, SLAB = 128, 352
UP, DOWN, LEFT, RIGHT, UL, UR, DL, DR = (
    (128, 48), (176, 48), (224, 32), (256, 32), (288, 16), (304, 16), (320, 16), (336, 16),
)


def iotas(shape):
    return lax.broadcasted_iota(jnp.int32, shape, 0), lax.broadcasted_iota(jnp.int32, shape, 1)


def pick(index, other):
    return jnp.where(index == other, 1.0, 0.0).astype(BF)


def pack_token(i):
    j = i & 31
    strip_col = j >> 3
    strip = (j & 7) * 16 + strip_col + jnp.where(i >= 32, 13, 0)
    strip = jnp.where(strip_col < 3, strip, -1)
    j = i & 15
    k = (i - 64) >> 4
    col, row = j >> 2, j & 3
    corner = (row + jnp.where(k >= 2, 5, 0)) * 16 + col + (k & 1) * 13
    corner = jnp.where(jnp.maximum(row, col) < 3, corner, -1)
    return jnp.where(i < 64, strip, corner)


def merge_token(i):
    t, s = i & 31, i >> 5
    return (2 * (t >> 3) + (s >> 1)) * 16 + 2 * (t & 7) + (s & 1)


def window_bias(up_ok, down_ok, left_ok, right_ok):
    i, lane = iotas((SLAB, 128))
    query_row, query_col = lane >> 4, lane & 15
    far = 1000
    j = i - 128
    edge_row = (j >> 4) + jnp.where(i < 176, -3, 5)
    edge_row = jnp.where(jnp.where(i < 176, up_ok, down_ok) > 0, edge_row, far)
    j = (i - 224) & 31
    strip_col = j >> 3
    strip_ok = jnp.where(i < 256, left_ok, right_ok) * jnp.where(strip_col < 3, 1, 0)
    strip_row = jnp.where(strip_ok > 0, j & 7, far)
    strip_col = strip_col + jnp.where(i < 256, -3, 16)
    j, k = (i - 288) & 15, (i - 288) >> 4
    col, row = j >> 2, j & 3
    corner_ok = jnp.where(k < 2, up_ok, down_ok) * jnp.where((k & 1) == 0, left_ok, right_ok)
    corner_ok = corner_ok * jnp.where(jnp.maximum(row, col) < 3, 1, 0)
    corner_row = jnp.where(corner_ok > 0, row + jnp.where(k < 2, -3, 8), far)
    corner_col = col + jnp.where((k & 1) == 0, -3, 16)
    key_row = jnp.where(
        i < 128, i >> 4, jnp.where(i < 224, edge_row, jnp.where(i < 288, strip_row, corner_row))
    )
    key_col = jnp.where(i < 224, i & 15, jnp.where(i < 288, strip_col, corner_col))
    gap = jnp.maximum(jnp.abs(key_row - query_row), jnp.abs(key_col - query_col))
    return jnp.where(gap <= 3, 0.0, NEG)


def dot(a, b):
    return jnp.dot(a, b, preferred_element_type=F32)


def dot_nt(a, b):
    return lax.dot_general(a, b, (((1,), (1,)), ((), ())), preferred_element_type=F32)


def dot_tn(a, b):
    return lax.dot_general(a, b, (((0,), (0,)), ((), ())), preferred_element_type=F32)


def softmax_rows(scores):
    highest = jnp.max(scores, 0, keepdims=True)
    expd = jnp.exp(scores - highest)
    return expd * (1.0 / jnp.sum(expd, 0, keepdims=True))


def phase(name, work):
    work()


class Guarded:
    def __init__(self, copy, sends, receives):
        self.copy, self.sends, self.receives = copy, sends, receives

    def start(self):
        pl.when(self.sends)(lambda: self.copy.start())

    def wait_send(self):
        pl.when(self.sends)(lambda: self.copy.wait_send())

    def wait_recv(self):
        pl.when(self.receives)(lambda: self.copy.wait_recv())


def kernel(
    rows, cols,
    fine_hbm, mw_hbm, cw_hbm, gain_hbm, cot_hbm,
    co_out, fg_out,
    fine, cot, gain_flat, mw, slab, pack, bias, hbias, probs, lse, attf, xm, qmsg, qpack, amsg, apack, qh, ah,
    w, nb, normed, cotp, gt, qbuf, kslab, vslab, pbuf, dsbuf, dsend, drecv, dqkv, osend, corecv,
    ngs, rs, mg, gown,
    fine_sem, cot_sem, gain_sem, mw_sem, hs, hr, qs, qr, gs, grs, ws, wr, wys, wfs, as_, ar, cs, cr, ks, kr, ds_, dr_, os_, orr, rss, rsr,
):
    row, col = lax.axis_index("row"), lax.axis_index("col")
    chip, core = col // 2, col % 2
    chips = cols // 2
    tokens = 32 * chips
    up, down = (row + rows - 1) % rows, (row + 1) % rows
    left, right = (col + cols - 1) % cols, (col + 1) % cols
    partner = col + 1 - 2 * core
    high, low_row = row // 4, row % 4
    ring = [4 * high + (low_row + j) % 4 for j in range(1, 4)]

    def remote(src, dst, send, recv, to_row, to_col):
        return pltpu.make_async_remote_copy(
            src_ref=src, dst_ref=dst, send_sem=send, recv_sem=recv,
            device_id=(to_row, to_col), device_id_type=MESH,
        )

    def part(ref, block):
        return ref.at[pl.ds(block[0], block[1])]

    barrier = pltpu.get_barrier_semaphore()
    for step in range(1, cols):
        pl.semaphore_signal(barrier, inc=1, device_id=(row, (col + step) % cols), device_id_type=MESH)
    for to_row in (up, down):
        for to_col in (left, col, right):
            pl.semaphore_signal(barrier, inc=1, device_id=(to_row, to_col), device_id_type=MESH)
    for to_row in ring:
        pl.semaphore_signal(barrier, inc=1, device_id=(to_row, col), device_id_type=MESH)

    load_fine = pltpu.make_async_copy(fine_hbm, fine, fine_sem)
    load_fine.start()
    load_cot = pltpu.make_async_copy(cot_hbm, cot, cot_sem)
    load_cot.start()
    load_gain = pltpu.make_async_copy(gain_hbm, gain_flat, gain_sem)
    load_gain.start()
    load = pltpu.make_async_copy(mw_hbm, mw, mw_sem)
    load.start()

    lane = lax.broadcasted_iota(jnp.int32, (1, 128), 1)
    even = jnp.where(lane < 64, 1.0, 0.0).astype(BF)
    odd = jnp.where(lane < 64, 0.0, 1.0).astype(BF)
    _, lanes = iotas((128, 128))

    def pack_all():
        i, t = iotas((128, 128))
        pack[...] = dot(pick(pack_token(i), t), fine[:, 768:2304]).astype(BF)
        for c in range(chips):
            cotp[c, :, 0:128] = cot[:, 128 * c : 128 * c + 128]
            at = 1024 + 64 * c
            cotp[c, :, 128:256] = jnp.concatenate([cot[:, at : at + 64], jnp.zeros((32, 64), BF)], 1)
        for kind in range(3):
            w[kind, 6:8] = jnp.zeros((2, 32, 1536), BF)

    load_fine.wait()
    load_cot.wait()
    load_gain.wait()
    gain = gain_flat[...].reshape(1, 1536)
    phase("pack", pack_all)

    for missing, blocks in (
        (row == 0, (UP, UL, UR)), (row == rows - 1, (DOWN, DL, DR)),
        (col == 0, (LEFT, UL, DL)), (col == cols - 1, (RIGHT, UR, DR)),
    ):

        @pl.when(missing)
        def _():
            for start, size in blocks:
                slab[start : start + size, :] = jnp.zeros((size, 1536), BF)
                for ref in (qh, ah):
                    ref[start - OWN : start - OWN + size, :] = jnp.zeros((size, 896), BF)

    pl.semaphore_wait(barrier, cols + 8)

    above, below, before, after = row > 0, row < rows - 1, col > 0, col < cols - 1

    def to_neighbours(rows_of, packed, into, send, recv):
        routes = [
            (rows_of(0), DOWN, up, col),
            (rows_of(80), UP, down, col),
            (packed.at[pl.ds(0, 32)], RIGHT, row, left),
            (packed.at[pl.ds(32, 32)], LEFT, row, right),
            (packed.at[pl.ds(64, 16)], DR, up, left),
            (packed.at[pl.ds(80, 16)], DL, up, right),
            (packed.at[pl.ds(96, 16)], UR, down, left),
            (packed.at[pl.ds(112, 16)], UL, down, right),
        ]
        sides = [
            (above, below), (below, above), (before, after), (after, before),
            (above & before, below & after), (above & after, below & before),
            (below & before, above & after), (below & after, above & before),
        ]
        return [
            Guarded(remote(src, into(block), send.at[n], recv.at[n], to_row, to_col), *sides[n])
            for n, (src, block, to_row, to_col) in enumerate(routes)
        ]

    def halo_rows(ref):
        return lambda block: ref.at[pl.ds(block[0] - OWN, block[1])]

    halo = to_neighbours(
        lambda at: fine.at[pl.ds(at, 48), pl.ds(768, 1536)], pack, lambda block: part(slab, block), hs, hr
    )
    for copy in halo:
        copy.start()

    chunks = []
    for k in range(9):
        chunk = 9 * col + k
        kind, place = chunk // 48, chunk % 48
        whole = place < 32
        to_chip = jnp.where(whole, place // 4, (place - 32) // 2)
        sub = jnp.where(whole, place % 4, 4 + place % 2)
        n = 6 * kind + sub
        to = 2 * to_chip + (n // 4) % 2
        src, dst = cw_hbm.at[pl.ds(32 * k, 32)], w.at[kind, sub]
        mine = n % 4 == low_row
        away = mine & (to != col)
        copy = remote(src, dst, ws.at[k], wr.at[n], row, to)
        chunks.append((away, copy))

        @pl.when(away)
        def _():
            copy.start()

        @pl.when(mine & (to == col))
        def _():
            pltpu.make_async_copy(src, dst, wr.at[n]).start()

    def slot(n):
        return w.at[n // 6, n % 6]

    def to_partner(n):
        return remote(slot(n), slot(n), wfs.at[n], wr.at[n], row, partner)

    def along_y(n):
        return [remote(slot(n), slot(n), wys.at[n, j], wr.at[n], ring[j], col) for j in range(3)]

    def each_part(of_core, places, work):
        for i in range(3):
            for place in places:
                n = 4 * (of_core + 2 * i) + place
                if i < 2:
                    work(n)
                else:

                    @pl.when(n < 18)
                    def _():
                        work(n)

    def wait_part(n):
        place = jnp.where(n % 6 < 4, 4 * chip + n % 6, 28 + 2 * chip + n % 6)
        source = (48 * (n // 6) + place) // 9

        @pl.when(source != col)
        def _():
            to_partner(n).wait_recv()

        @pl.when(source == col)
        def _():
            pltpu.make_async_copy(cw_hbm.at[pl.ds(0, 32)], slot(n), wr.at[n]).wait()

    cot_copies = [
        remote(cotp.at[(chip + d) % chips], gt.at[d], cs.at[d], cr.at[d], row, 2 * ((chip + d) % chips) + core)
        for d in range(1, chips)
    ]
    gt[0] = cotp[chip]

    def window_all():
        slab[0:OWN, :] = fine[:, 768:2304]
        window = window_bias(
            jnp.where(row > 0, 1, 0), jnp.where(row < rows - 1, 1, 0),
            jnp.where(col > 0, 1, 0), jnp.where(col < cols - 1, 1, 0),
        )
        bias[:, 0:128] = window
        bias[:, 128:256] = window
        outer = jnp.concatenate([window[OWN:SLAB], jnp.full((32, 128), NEG, F32)], 0).T
        hbias[:, 0:256] = outer
        hbias[:, 256:512] = outer
        for ref in (qh, ah):
            ref[224:256, :] = jnp.zeros((32, 896), BF)

    phase("window", window_all)

    def both_heads(block):
        return jnp.concatenate([block * even, block * odd], 0)

    def own_lanes(two):
        return jnp.where(lanes < 64, two[0:128], two[128:256])

    for copy in halo:
        copy.wait_recv()

    for copy in cot_copies:
        copy.start()

    def fine_forward():
        lse[12:16, :] = jnp.zeros((4, 128), F32)
        outs = []
        for p in range(6):
            at = 128 * p
            query = both_heads(fine[:, at : at + 128] * SCALE)
            scores = dot_nt(slab[:, at : at + 128], query) + bias[...]
            highest = jnp.max(scores, 0, keepdims=True)
            expd = jnp.exp(scores - highest)
            total = jnp.sum(expd, 0, keepdims=True)
            weights = (expd * (1.0 / total)).astype(BF)
            probs[p] = weights
            norm = highest + jnp.log(total)
            lse[2 * p : 2 * p + 1, :] = norm[:, 0:128]
            lse[2 * p + 1 : 2 * p + 2, :] = norm[:, 128:256]
            out = own_lanes(dot_tn(weights, slab[:, 768 + at : 768 + at + 128]))
            attf[:, at : at + 128] = out
            outs.append(out.astype(BF))
        i, t = iotas((128, 128))
        xm[...] = dot(pick(merge_token(i), t), jnp.concatenate(outs, 1)).astype(BF)

    phase("fine_forward", fine_forward)
    def pass_on(n):
        wait_part(n)
        for copy in along_y(n):
            copy.start()
        to_partner(n).start()

    each_part(core, [low_row], pass_on)
    load.wait()

    def normalise(d):
        wide = jnp.concatenate([nb[0, d], nb[1, d]], 1).astype(F32)
        inverse = lax.rsqrt(jnp.mean(wide * wide, -1, keepdims=True) + 1e-06)
        normed[32 * d : 32 * d + 32, :] = (wide * inverse * gain).astype(BF)

    gather = []
    for half in range(2):

        def merge():
            at = slice(768 * half, 768 * half + 768)
            total = dot(xm[0:32, :], mw[0:768, at])
            for s in range(1, 4):
                total = total + dot(xm[32 * s : 32 * s + 32, :], mw[768 * s : 768 * s + 768, at])
            nb[half, 0] = total.astype(BF)

        phase("merge", merge)
        copies = [
            remote(
                nb.at[half, 0], nb.at[half, d], as_.at[half, d], ar.at[half, d],
                row, 2 * ((chip + d) % chips) + core,
            )
            for d in range(1, chips)
        ]
        for copy in copies:
            copy.start()
        gather.append(copies)
    normalise(0)

    def query_message():
        norm = lse[...]
        high = norm.astype(BF).astype(F32)
        middle = (norm - high).astype(BF).astype(F32)
        terms = [high, middle, norm - high - middle, jnp.zeros((80, 128), F32)]
        qmsg[:, 0:768] = fine[:, 0:768]
        qmsg[:, 768:896] = jnp.concatenate(terms, 0).T.astype(BF)
        i, t = iotas((128, 128))
        qpack[...] = dot(pick(pack_token(i), t), qmsg[...]).astype(BF)

    phase("query_message", query_message)
    def pass_over(n):
        to_partner(n).wait_recv()
        to_partner(n).start()

    each_part(core, [(low_row + j) % 4 for j in range(1, 4)], pass_over)

    for d in range(1, chips):
        gather[0][d - 1].wait_recv()
        gather[1][d - 1].wait_recv()
        normalise(d)
    each_part(1 - core, range(4), lambda n: to_partner(n).wait_recv())

    def project(kind):
        return dot_nt(normed[...], w[kind].reshape(256, 1536)).astype(BF)

    def project_keys():
        kslab[0:tokens, :] = project(1)

    def project_values():
        vslab[0:tokens, :] = project(2)

    def project_query():
        qbuf[...] = project(0)

    phase("project_k", project_keys)
    swap_k = remote(kslab.at[pl.ds(0, tokens)], kslab.at[pl.ds(tokens, tokens)], ks.at[0], kr.at[0], row, partner)
    swap_k.start()
    phase("project_v", project_values)
    swap_v = remote(vslab.at[pl.ds(0, tokens)], vslab.at[pl.ds(tokens, tokens)], ks.at[1], kr.at[1], row, partner)
    swap_v.start()
    rim_queries = to_neighbours(lambda at: qmsg.at[pl.ds(at, 48)], qpack, halo_rows(qh), qs, qr)
    for copy in rim_queries:
        copy.start()
    phase("project_q", project_query)
    for copy in cot_copies:
        copy.wait_recv()
    swap_k.wait_recv()
    swap_v.wait_recv()
    wide_lane = lax.broadcasted_iota(jnp.int32, (tokens, 128), 1)

    def head_refs(head):
        at = 128 * (head // 2)
        mask = (even, odd, even)[head]
        query = qbuf[:, at : at + 128] * mask * SCALE
        grad = gt[:, :, at : at + 128].reshape(tokens, 128) * mask
        return query, grad, kslab[:, at : at + 128], vslab[:, at : at + 128]

    def key_grads(low):
        span = slice(low, low + tokens)
        dks, dvs = [], []
        for head in range(3):
            query, grad, _, _ = head_refs(head)
            dks.append(dot(dsbuf[head, span, :], query))
            dvs.append(dot(pbuf[head, span, :], grad))
        return [jnp.concatenate([d[0] + d[1], d[2]], 1) for d in (dks, dvs)]

    def band():
        for head in range(3):
            query, grad, keys, values = head_refs(head)
            weights = softmax_rows(dot_nt(keys, query))
            pbuf[head] = weights.astype(BF)
            dp = dot_nt(values, grad)
            delta = jnp.sum(weights * dp, 0, keepdims=True)
            dsbuf[head] = (weights * (dp - delta)).astype(BF)
        for which, both in enumerate(key_grads(tokens)):
            dsend[which] = both.astype(BF)

    phase("band", band)
    swap_d = remote(dsend, drecv, ds_, dr_, row, partner)
    swap_d.start()

    def band_rest():
        outs, dqs = [], []
        for head in range(3):
            _, _, keys, values = head_refs(head)
            dqs.append(dot_tn(dsbuf[head], keys) * SCALE)
            outs.append(dot_tn(pbuf[head], values))
        dqkv[:, 0:128] = jnp.where(wide_lane < 64, dqs[0], dqs[1]).astype(BF)
        dqkv[:, 128:256] = dqs[2].astype(BF)
        out = jnp.concatenate([jnp.where(wide_lane < 64, outs[0], outs[1]), outs[2]], 1)
        osend[...] = out.astype(BF).reshape(chips, 32, 256)
        corecv[chip] = osend[0]

    phase("band_rest", band_rest)
    out_copies = [
        remote(osend.at[d], corecv.at[chip], os_.at[d], orr.at[d], row, 2 * ((chip + chips - d) % chips) + core)
        for d in range(1, chips)
    ]
    own_grads = key_grads(0)
    swap_d.wait_recv()
    for which in range(2):
        at = 256 + 256 * which
        dqkv[:, at : at + 256] = (own_grads[which] + drecv[which].astype(F32)).astype(BF)

    scatter = []
    for half in (1, 0):
        first = half * (chips // 2)
        span = slice(first * 32, first * 32 + tokens // 2)

        def back_project():
            for n in range(3):
                at = slice(512 * n, 512 * n + 512)
                total = dot(dqkv[span, :], w[:, :, :, at].reshape(768, 512))
                ngs[first : first + chips // 2, :, at] = total.astype(BF).reshape(chips // 2, 32, 512)

        phase("back_project", back_project)
        copies = [
            remote(ngs.at[d], rs.at[d], rss.at[d], rsr.at[d], row, 2 * ((chip + chips - d) % chips) + core)
            for d in range(max(first, 1), first + chips // 2)
        ]
        for copy in copies:
            copy.start()
        scatter += copies
    for copy in scatter:
        copy.wait_recv()

    def unmerge():
        total = ngs[0].astype(F32)
        for d in range(1, chips):
            total = total + rs[d].astype(F32)
        wide = jnp.concatenate([nb[0, 0], nb[1, 0]], 1).astype(F32)
        inverse = lax.rsqrt(jnp.mean(wide * wide, -1, keepdims=True) + 1e-06)
        scaled = total * gain
        cgrad = inverse * (scaled - wide * (inverse * inverse * jnp.mean(scaled * wide, -1, keepdims=True)))
        cgrad = cgrad.astype(BF)

        for n in range(3):
            at = slice(1024 * n, 1024 * n + 1024)
            mg[at, :] = dot_nt(mw[at, :], cgrad).astype(BF)
        token, t = iotas((128, 32))
        total = jnp.zeros((128, 768), F32)
        for s in range(4):
            total = total + dot_nt(pick(merge_token(32 * s + t), token), mg[768 * s : 768 * s + 768, :])
        amsg[:, 0:768] = total.astype(BF)
        product = amsg[:, 0:768].astype(F32) * attf[...]
        feature, lane_of = iotas((768, 128))
        heads = jnp.where(lane_of < 32, pick(feature >> 6, lane_of & 15).astype(F32), 0.0).astype(BF)
        high = product.astype(BF)
        delta = dot(high, heads) + dot((product - high.astype(F32)).astype(BF), heads)
        high = delta.astype(BF).astype(F32)
        amsg[:, 768:896] = jnp.where(lanes < 16, high, delta - high).astype(BF)
        i, t = iotas((128, 128))
        apack[...] = dot(pick(pack_token(i), t), amsg[...]).astype(BF)

    phase("unmerge", unmerge)

    rim_grads = to_neighbours(lambda at: amsg.at[pl.ds(at, 48)], apack, halo_rows(ah), gs, grs)
    for copy in rim_grads:
        copy.start()
    for copy in out_copies:
        copy.start()

    def fine_backward_own():
        for p in range(6):
            at = 128 * p
            query = both_heads(fine[:, at : at + 128] * SCALE)
            grad = both_heads(amsg[:, at : at + 128])
            weights_low = probs[p]
            weights = weights_low.astype(F32)
            dp = dot_nt(slab[:, 768 + at : 768 + at + 128], grad)
            delta = jnp.sum(weights * dp, 0, keepdims=True)
            ds_low = (weights * (dp - delta)).astype(BF)
            gown[:, at : at + 128] = dot(ds_low[0:OWN], query)
            gown[:, 768 + at : 768 + at + 128] = dot(weights_low[0:OWN], grad)
            dq = dot_tn(ds_low, slab[:, at : at + 128]) * SCALE
            fg_out[:, at : at + 128] = own_lanes(dq).astype(BF)

    phase("fine_back_own", fine_backward_own)

    for copy in rim_queries:
        copy.wait_recv()
    terms = qh[:, 768:896].astype(F32).T
    rim_lse = terms[0:16] + terms[16:32] + terms[32:48]
    for copy in rim_grads:
        copy.wait_recv()

    def fine_backward_rim():
        terms = ah[:, 768:896].astype(F32).T
        rim_delta = terms[0:16] + terms[16:32]

        def row_of(stat, p):
            return jnp.concatenate([stat[2 * p : 2 * p + 1], stat[2 * p + 1 : 2 * p + 2]], 1)

        for p in range(6):
            at, val = 128 * p, 768 + 128 * p
            query = both_heads(qh[:, at : at + 128] * SCALE)
            grad = both_heads(ah[:, at : at + 128])
            scores = dot_nt(slab[0:OWN, at : at + 128], query) + hbias[...]
            weights = jnp.exp(scores - row_of(rim_lse, p))
            dp = dot_nt(slab[0:OWN, val : val + 128], grad)
            ds_low = (weights * (dp - row_of(rim_delta, p))).astype(BF)
            dk = gown[:, at : at + 128] + dot(ds_low, query)
            dv = gown[:, val : val + 128] + dot(weights.astype(BF), grad)
            fg_out[:, 768 + at : 896 + at] = dk.astype(BF)
            fg_out[:, 768 + val : 896 + val] = dv.astype(BF)

    phase("fine_back_rim", fine_backward_rim)
    for d in range(1, chips):
        source = (chip + d) % chips
        remote(osend.at[d], corecv.at[source], os_.at[d], orr.at[d], row, 2 * source + core).wait_recv()

    def coarse_output():
        for c in range(chips):
            co_out[:, 128 * c : 128 * c + 128] = corecv[c, :, 0:128]
        for c in range(0, chips, 2):
            at = 1024 + 64 * c
            co_out[:, at : at + 128] = jnp.concatenate([corecv[c, :, 128:192], corecv[c + 1, :, 128:192]], 1)

    phase("coarse_output", coarse_output)
    for copy in halo + cot_copies + gather[0] + gather[1] + [swap_k, swap_v, swap_d] + out_copies + scatter + rim_queries + rim_grads:
        copy.wait_send()
    for away, copy in chunks:

        @pl.when(away)
        def _():
            copy.wait_send()

    def sent_along_y(n):
        for copy in along_y(n):
            copy.wait_send()

    each_part(core, range(4), lambda n: to_partner(n).wait_send())
    each_part(core, [low_row], sent_along_y)


def carry(a, b, a_out, b_out):
    a_out[...] = a[...]
    b_out[...] = b[...]


def shards(mesh_rows, mesh_cols, fine_qkv, merge_weight, coarse_weight, norm_gain, cotangent):
    chips = mesh_cols // 2
    tokens = 32 * chips
    vmem = pl.BlockSpec(memory_space=pltpu.VMEM)
    hbm = pl.BlockSpec(memory_space=pl.ANY)
    dma = pltpu.SemaphoreType.DMA

    def low(*shape):
        return pltpu.VMEM(shape, BF)

    def full(*shape):
        return pltpu.VMEM(shape, F32)

    coarse_out, fine_grad = pl.pallas_call(
        functools.partial(kernel, mesh_rows, mesh_cols),
        out_shape=(jax.ShapeDtypeStruct((32, 1536), BF), jax.ShapeDtypeStruct((128, 2304), BF)),
        in_specs=[hbm] * 5,
        out_specs=(vmem, vmem),
        scratch_shapes=[
            low(128, 2304), low(32, 1536), full(1536), low(3072, 1536), low(SLAB, 1536), low(128, 1536), full(SLAB, 256),
            full(128, 512), low(6, SLAB, 256),
            full(16, 128), full(128, 768), low(128, 768),
            low(128, 896), low(128, 896), low(128, 896), low(128, 896), low(256, 896), low(256, 896),
            low(3, 8, 32, 1536), low(2, chips, 32, 768), low(tokens, 1536),
            low(chips, 32, 256), low(chips, 32, 256), low(tokens, 256), low(2 * tokens, 256),
            low(2 * tokens, 256), low(3, 2 * tokens, tokens), low(3, 2 * tokens, tokens), low(2, tokens, 256), low(2, tokens, 256), low(tokens, 768),
            low(chips, 32, 256), low(chips, 32, 256),
            low(chips, 32, 1536), low(chips, 32, 1536), low(3072, 32), full(128, 1536),
            dma, dma, dma, dma, dma((8,)), dma((8,)), dma((8,)), dma((8,)), dma((8,)), dma((8,)), dma((9,)), dma((18,)),
            dma((18, 3)), dma((18,)), dma((2, chips)), dma((2, chips)), dma((chips,)), dma((chips,)),
            dma((2,)), dma((2,)), dma, dma, dma((chips,)), dma((chips,)), dma((chips,)), dma((chips,)),
        ],
        compiler_params=pltpu.CompilerParams(
            collective_id=0, has_side_effects=True, vmem_limit_bytes=56 * 1024 * 1024
        ),
    )(
        fine_qkv.reshape(128, 2304),
        merge_weight,
        coarse_weight.T,
        norm_gain,
        cotangent.reshape(32, 1536),
    )
    coarse_out, fine_grad = pl.pallas_call(
        carry,
        out_shape=(jax.ShapeDtypeStruct((32, 1536), BF), jax.ShapeDtypeStruct((128, 2304), BF)),
        in_specs=[vmem, vmem],
        out_specs=(vmem, vmem),
    )(coarse_out, fine_grad)
    return coarse_out.reshape(4, 8, 1536), fine_grad.reshape(8, 16, 2304)


def solution(mesh):
    placed = (P("row", "col", None), P(), P(None, "col"), P(), P("row", "col", None))
    return jax.shard_map(
        functools.partial(shards, mesh.shape["row"], mesh.shape["col"]),
        mesh=mesh,
        in_specs=placed,
        out_specs=(P("row", "col", None), P("row", "col", None)),
        check_vma=False,
    )
```

```python
import functools

import jax
import jax.numpy as jnp
from jax import lax
from jax.experimental import pallas as pl
from jax.experimental.pallas import tpu as pltpu
from jax.sharding import PartitionSpec as P

MESH = pl.DeviceIdType.MESH
BF = jnp.bfloat16
F32 = jnp.float32
HD = 64
SCALE = HD ** (-0.5)
NEG = -1e30

OWN, SLAB = 128, 352
UP, DOWN, LEFT, RIGHT, UL, UR, DL, DR = (
    (128, 48), (176, 48), (224, 32), (256, 32), (288, 16), (304, 16), (320, 16), (336, 16),
)


def iotas(shape):
    return lax.broadcasted_iota(jnp.int32, shape, 0), lax.broadcasted_iota(jnp.int32, shape, 1)


def pick(index, other):
    return jnp.where(index == other, 1.0, 0.0).astype(BF)


def pack_token(i):
    j = i & 31
    strip_col = j >> 3
    strip = (j & 7) * 16 + strip_col + jnp.where(i >= 32, 13, 0)
    strip = jnp.where(strip_col < 3, strip, -1)
    j = i & 15
    k = (i - 64) >> 4
    col, row = j >> 2, j & 3
    corner = (row + jnp.where(k >= 2, 5, 0)) * 16 + col + (k & 1) * 13
    corner = jnp.where(jnp.maximum(row, col) < 3, corner, -1)
    return jnp.where(i < 64, strip, corner)


def merge_token(i):
    t, s = i & 31, i >> 5
    return (2 * (t >> 3) + (s >> 1)) * 16 + 2 * (t & 7) + (s & 1)


def window_bias(up_ok, down_ok, left_ok, right_ok):
    i, lane = iotas((SLAB, 128))
    query_row, query_col = lane >> 4, lane & 15
    far = 1000
    j = i - 128
    edge_row = (j >> 4) + jnp.where(i < 176, -3, 5)
    edge_row = jnp.where(jnp.where(i < 176, up_ok, down_ok) > 0, edge_row, far)
    j = (i - 224) & 31
    strip_col = j >> 3
    strip_ok = jnp.where(i < 256, left_ok, right_ok) * jnp.where(strip_col < 3, 1, 0)
    strip_row = jnp.where(strip_ok > 0, j & 7, far)
    strip_col = strip_col + jnp.where(i < 256, -3, 16)
    j, k = (i - 288) & 15, (i - 288) >> 4
    col, row = j >> 2, j & 3
    corner_ok = jnp.where(k < 2, up_ok, down_ok) * jnp.where((k & 1) == 0, left_ok, right_ok)
    corner_ok = corner_ok * jnp.where(jnp.maximum(row, col) < 3, 1, 0)
    corner_row = jnp.where(corner_ok > 0, row + jnp.where(k < 2, -3, 8), far)
    corner_col = col + jnp.where((k & 1) == 0, -3, 16)
    key_row = jnp.where(
        i < 128, i >> 4, jnp.where(i < 224, edge_row, jnp.where(i < 288, strip_row, corner_row))
    )
    key_col = jnp.where(i < 224, i & 15, jnp.where(i < 288, strip_col, corner_col))
    gap = jnp.maximum(jnp.abs(key_row - query_row), jnp.abs(key_col - query_col))
    return jnp.where(gap <= 3, 0.0, NEG)


def dot(a, b):
    return jnp.dot(a, b, preferred_element_type=F32)


def dot_nt(a, b):
    return lax.dot_general(a, b, (((1,), (1,)), ((), ())), preferred_element_type=F32)


def dot_tn(a, b):
    return lax.dot_general(a, b, (((0,), (0,)), ((), ())), preferred_element_type=F32)


def softmax_rows(scores):
    highest = jnp.max(scores, 0, keepdims=True)
    expd = jnp.exp(scores - highest)
    return expd * (1.0 / jnp.sum(expd, 0, keepdims=True))


def phase(name, work):
    work()


class Guarded:
    def __init__(self, copy, sends, receives):
        self.copy, self.sends, self.receives = copy, sends, receives

    def start(self):
        pl.when(self.sends)(lambda: self.copy.start())

    def wait_send(self):
        pl.when(self.sends)(lambda: self.copy.wait_send())

    def wait_recv(self):
        pl.when(self.receives)(lambda: self.copy.wait_recv())


def kernel(
    rows, cols,
    fine_hbm, mw_hbm, cw_hbm, gain_hbm, cot_hbm,
    co_hbm, fg_hbm,
    co_out, fg_out, fine, cot, gain_flat, mw, slab, pack, bias, hbias, probs, prim, lse, attf, xm, qmsg, qpack, amsg, apack, qh, ah,
    w, nb, normed, cotp, gt, qbuf, kslab, vslab, pbuf, dsbuf, dsend, drecv, dqkv, osend, corecv,
    ngs, rs, mg, gown,
    fine_sem, cot_sem, gain_sem, mw_sem, co_sem, dq_sem, kv_sem, hs, hr, qs, qr, gs, grs, ws, wr, wys, wfs, as_, ar, cs, cr, ks, kr, ds_, dr_, os_, orr, rss, rsr,
):
    row, col = lax.axis_index("row"), lax.axis_index("col")
    chip, core = col // 2, col % 2
    chips = cols // 2
    tokens = 32 * chips
    up, down = (row + rows - 1) % rows, (row + 1) % rows
    left, right = (col + cols - 1) % cols, (col + 1) % cols
    partner = col + 1 - 2 * core
    high, low_row = row // 4, row % 4
    ring = [4 * high + (low_row + j) % 4 for j in range(1, 4)]

    def remote(src, dst, send, recv, to_row, to_col):
        return pltpu.make_async_remote_copy(
            src_ref=src, dst_ref=dst, send_sem=send, recv_sem=recv,
            device_id=(to_row, to_col), device_id_type=MESH,
        )

    def part(ref, block):
        return ref.at[pl.ds(block[0], block[1])]

    barrier = pltpu.get_barrier_semaphore()
    for step in range(1, cols):
        pl.semaphore_signal(barrier, inc=1, device_id=(row, (col + step) % cols), device_id_type=MESH)
    for to_row in (up, down):
        for to_col in (left, col, right):
            pl.semaphore_signal(barrier, inc=1, device_id=(to_row, to_col), device_id_type=MESH)
    for to_row in ring:
        pl.semaphore_signal(barrier, inc=1, device_id=(to_row, col), device_id_type=MESH)

    load_fine = pltpu.make_async_copy(fine_hbm, fine, fine_sem)
    load_fine.start()
    load_cot = pltpu.make_async_copy(cot_hbm, cot, cot_sem)
    load_cot.start()
    load_gain = pltpu.make_async_copy(gain_hbm, gain_flat, gain_sem)
    load_gain.start()
    load = pltpu.make_async_copy(mw_hbm, mw, mw_sem)
    load.start()

    lane = lax.broadcasted_iota(jnp.int32, (1, 128), 1)
    even = jnp.where(lane < 64, 1.0, 0.0).astype(BF)
    odd = jnp.where(lane < 64, 0.0, 1.0).astype(BF)
    _, lanes = iotas((128, 128))

    def pack_all():
        i, t = iotas((128, 128))
        pack[...] = dot(pick(pack_token(i), t), fine[:, 768:2304]).astype(BF)
        for c in range(chips):
            cotp[c, :, 0:128] = cot[:, 128 * c : 128 * c + 128]
            at = 1024 + 64 * c
            cotp[c, :, 128:256] = jnp.concatenate([cot[:, at : at + 64], jnp.zeros((32, 64), BF)], 1)
        for kind in range(3):
            w[kind, 6:8] = jnp.zeros((2, 32, 1536), BF)

    load_fine.wait()
    load_cot.wait()
    load_gain.wait()
    gain = gain_flat[...].reshape(1, 1536)
    phase("pack", pack_all)

    for missing, blocks in (
        (row == 0, (UP, UL, UR)), (row == rows - 1, (DOWN, DL, DR)),
        (col == 0, (LEFT, UL, DL)), (col == cols - 1, (RIGHT, UR, DR)),
    ):

        @pl.when(missing)
        def _():
            for start, size in blocks:
                slab[start : start + size, :] = jnp.zeros((size, 1536), BF)
                for ref in (qh, ah):
                    ref[start - OWN : start - OWN + size, :] = jnp.zeros((size, 896), BF)

    pl.semaphore_wait(barrier, cols + 8)

    above, below, before, after = row > 0, row < rows - 1, col > 0, col < cols - 1

    def to_neighbours(rows_of, packed, into, send, recv):
        routes = [
            (rows_of(0), DOWN, up, col),
            (rows_of(80), UP, down, col),
            (packed.at[pl.ds(0, 32)], RIGHT, row, left),
            (packed.at[pl.ds(32, 32)], LEFT, row, right),
            (packed.at[pl.ds(64, 16)], DR, up, left),
            (packed.at[pl.ds(80, 16)], DL, up, right),
            (packed.at[pl.ds(96, 16)], UR, down, left),
            (packed.at[pl.ds(112, 16)], UL, down, right),
        ]
        sides = [
            (above, below), (below, above), (before, after), (after, before),
            (above & before, below & after), (above & after, below & before),
            (below & before, above & after), (below & after, above & before),
        ]
        return [
            Guarded(remote(src, into(block), send.at[n], recv.at[n], to_row, to_col), *sides[n])
            for n, (src, block, to_row, to_col) in enumerate(routes)
        ]

    def halo_rows(ref):
        return lambda block: ref.at[pl.ds(block[0] - OWN, block[1])]

    halo = to_neighbours(
        lambda at: fine.at[pl.ds(at, 48), pl.ds(768, 1536)], pack, lambda block: part(slab, block), hs, hr
    )
    for copy in halo:
        copy.start()

    chunks = []
    for k in range(9):
        chunk = 9 * col + k
        kind, place = chunk // 48, chunk % 48
        whole = place < 32
        to_chip = jnp.where(whole, place // 4, (place - 32) // 2)
        sub = jnp.where(whole, place % 4, 4 + place % 2)
        n = 6 * kind + sub
        to = 2 * to_chip + (n // 4) % 2
        src, dst = cw_hbm.at[pl.ds(32 * k, 32)], w.at[kind, sub]
        mine = n % 4 == low_row
        away = mine & (to != col)
        copy = remote(src, dst, ws.at[k], wr.at[n], row, to)
        chunks.append((away, copy))

        @pl.when(away)
        def _():
            copy.start()

        @pl.when(mine & (to == col))
        def _():
            pltpu.make_async_copy(src, dst, wr.at[n]).start()

    def slot(n):
        return w.at[n // 6, n % 6]

    def to_partner(n):
        return remote(slot(n), slot(n), wfs.at[n], wr.at[n], row, partner)

    def along_y(n):
        return [remote(slot(n), slot(n), wys.at[n, j], wr.at[n], ring[j], col) for j in range(3)]

    def each_part(of_core, places, work):
        for i in range(3):
            for place in places:
                n = 4 * (of_core + 2 * i) + place
                if i < 2:
                    work(n)
                else:

                    @pl.when(n < 18)
                    def _():
                        work(n)

    def wait_part(n):
        place = jnp.where(n % 6 < 4, 4 * chip + n % 6, 28 + 2 * chip + n % 6)
        source = (48 * (n // 6) + place) // 9

        @pl.when(source != col)
        def _():
            to_partner(n).wait_recv()

        @pl.when(source == col)
        def _():
            pltpu.make_async_copy(cw_hbm.at[pl.ds(0, 32)], slot(n), wr.at[n]).wait()

    cot_copies = [
        remote(cotp.at[(chip + d) % chips], gt.at[d], cs.at[d], cr.at[d], row, 2 * ((chip + d) % chips) + core)
        for d in range(1, chips)
    ]
    gt[0] = cotp[chip]

    def window_all():
        slab[0:OWN, :] = fine[:, 768:2304]
        window = window_bias(
            jnp.where(row > 0, 1, 0), jnp.where(row < rows - 1, 1, 0),
            jnp.where(col > 0, 1, 0), jnp.where(col < cols - 1, 1, 0),
        )
        bias[:, 0:128] = window
        bias[:, 128:256] = window
        outer = jnp.concatenate([window[OWN:SLAB], jnp.full((32, 128), NEG, F32)], 0).T
        hbias[:, 0:256] = outer
        hbias[:, 256:512] = outer
        for ref in (qh, ah):
            ref[224:256, :] = jnp.zeros((32, 896), BF)

    phase("window", window_all)

    def both_heads(block):
        return jnp.concatenate([block * even, block * odd], 0)

    def own_lanes(two):
        return jnp.where(lanes < 64, two[0:128], two[128:256])

    for copy in halo:
        copy.wait_recv()

    for copy in cot_copies:
        copy.start()

    def fine_forward():
        lse[12:16, :] = jnp.zeros((4, 128), F32)
        outs = []
        for p in range(6):
            at = 128 * p
            query = both_heads(fine[:, at : at + 128] * SCALE)
            scores = dot_nt(slab[:, at : at + 128], query) + bias[...]
            highest = jnp.max(scores, 0, keepdims=True)
            expd = jnp.exp(scores - highest)
            total = jnp.sum(expd, 0, keepdims=True)
            weights = (expd * (1.0 / total)).astype(BF)
            probs[p] = weights
            norm = highest + jnp.log(total)
            lse[2 * p : 2 * p + 1, :] = norm[:, 0:128]
            lse[2 * p + 1 : 2 * p + 2, :] = norm[:, 128:256]
            out = own_lanes(dot_tn(weights, slab[:, 768 + at : 768 + at + 128]))
            attf[:, at : at + 128] = out
            outs.append(out.astype(BF))
        i, t = iotas((128, 128))
        xm[...] = dot(pick(merge_token(i), t), jnp.concatenate(outs, 1)).astype(BF)

    phase("fine_forward", fine_forward)
    def pass_on(n):
        wait_part(n)
        for copy in along_y(n):
            copy.start()
        to_partner(n).start()

    each_part(core, [low_row], pass_on)
    load.wait()

    def normalise(d):
        wide = jnp.concatenate([nb[0, d], nb[1, d]], 1).astype(F32)
        inverse = lax.rsqrt(jnp.mean(wide * wide, -1, keepdims=True) + 1e-06)
        normed[32 * d : 32 * d + 32, :] = (wide * inverse * gain).astype(BF)

    gather = []
    for half in range(2):

        def merge():
            at = slice(768 * half, 768 * half + 768)
            total = dot(xm[0:32, :], mw[0:768, at])
            for s in range(1, 4):
                total = total + dot(xm[32 * s : 32 * s + 32, :], mw[768 * s : 768 * s + 768, at])
            nb[half, 0] = total.astype(BF)

        phase("merge", merge)
        copies = [
            remote(
                nb.at[half, 0], nb.at[half, d], as_.at[half, d], ar.at[half, d],
                row, 2 * ((chip + d) % chips) + core,
            )
            for d in range(1, chips)
        ]
        for copy in copies:
            copy.start()
        gather.append(copies)
    normalise(0)

    def query_message():
        norm = lse[...]
        high = norm.astype(BF).astype(F32)
        middle = (norm - high).astype(BF).astype(F32)
        terms = [high, middle, norm - high - middle, jnp.zeros((80, 128), F32)]
        qmsg[:, 0:768] = fine[:, 0:768]
        qmsg[:, 768:896] = jnp.concatenate(terms, 0).T.astype(BF)
        i, t = iotas((128, 128))
        qpack[...] = dot(pick(pack_token(i), t), qmsg[...]).astype(BF)

    phase("query_message", query_message)
    def pass_over(n):
        to_partner(n).wait_recv()
        to_partner(n).start()

    each_part(core, [(low_row + j) % 4 for j in range(1, 4)], pass_over)

    for d in range(1, chips):
        gather[0][d - 1].wait_recv()
        gather[1][d - 1].wait_recv()
        normalise(d)
    each_part(1 - core, range(4), lambda n: to_partner(n).wait_recv())

    def project(kind):
        return dot_nt(normed[...], w[kind].reshape(256, 1536)).astype(BF)

    def project_keys():
        kslab[0:tokens, :] = project(1)

    def project_values():
        vslab[0:tokens, :] = project(2)

    def project_query():
        qbuf[...] = project(0)

    phase("project_k", project_keys)
    swap_k = remote(kslab.at[pl.ds(0, tokens)], kslab.at[pl.ds(tokens, tokens)], ks.at[0], kr.at[0], row, partner)
    swap_k.start()
    phase("project_v", project_values)
    swap_v = remote(vslab.at[pl.ds(0, tokens)], vslab.at[pl.ds(tokens, tokens)], ks.at[1], kr.at[1], row, partner)
    swap_v.start()
    rim_queries = to_neighbours(lambda at: qmsg.at[pl.ds(at, 48)], qpack, halo_rows(qh), qs, qr)
    for copy in rim_queries:
        copy.start()
    phase("project_q", project_query)
    for copy in cot_copies:
        copy.wait_recv()
    swap_k.wait_recv()
    swap_v.wait_recv()
    wide_lane = lax.broadcasted_iota(jnp.int32, (tokens, 128), 1)

    def head_refs(head):
        at = 128 * (head // 2)
        mask = (even, odd, even)[head]
        query = qbuf[:, at : at + 128] * mask * SCALE
        grad = gt[:, :, at : at + 128].reshape(tokens, 128) * mask
        return query, grad, kslab[:, at : at + 128], vslab[:, at : at + 128]

    def key_grads(low):
        span = slice(low, low + tokens)
        dks, dvs = [], []
        for head in range(3):
            query, grad, _, _ = head_refs(head)
            dks.append(dot(dsbuf[head, span, :], query))
            dvs.append(dot(pbuf[head, span, :], grad))
        return [jnp.concatenate([d[0] + d[1], d[2]], 1) for d in (dks, dvs)]

    def band():
        for head in range(3):
            query, grad, keys, values = head_refs(head)
            weights = softmax_rows(dot_nt(keys, query))
            pbuf[head] = weights.astype(BF)
            dp = dot_nt(values, grad)
            delta = jnp.sum(weights * dp, 0, keepdims=True)
            dsbuf[head] = (weights * (dp - delta)).astype(BF)
        for which, both in enumerate(key_grads(tokens)):
            dsend[which] = both.astype(BF)

    phase("band", band)
    swap_d = remote(dsend, drecv, ds_, dr_, row, partner)
    swap_d.start()

    def band_rest():
        outs, dqs = [], []
        for head in range(3):
            _, _, keys, values = head_refs(head)
            dqs.append(dot_tn(dsbuf[head], keys) * SCALE)
            outs.append(dot_tn(pbuf[head], values))
        dqkv[:, 0:128] = jnp.where(wide_lane < 64, dqs[0], dqs[1]).astype(BF)
        dqkv[:, 128:256] = dqs[2].astype(BF)
        out = jnp.concatenate([jnp.where(wide_lane < 64, outs[0], outs[1]), outs[2]], 1)
        osend[...] = out.astype(BF).reshape(chips, 32, 256)
        corecv[chip] = osend[0]

    phase("band_rest", band_rest)
    out_copies = [
        remote(osend.at[d], corecv.at[chip], os_.at[d], orr.at[d], row, 2 * ((chip + chips - d) % chips) + core)
        for d in range(1, chips)
    ]
    own_grads = key_grads(0)
    swap_d.wait_recv()
    for which in range(2):
        at = 256 + 256 * which
        dqkv[:, at : at + 256] = (own_grads[which] + drecv[which].astype(F32)).astype(BF)

    scatter = []
    for half in (1, 0):
        first = half * (chips // 2)
        span = slice(first * 32, first * 32 + tokens // 2)

        def back_project():
            for n in range(3):
                at = slice(512 * n, 512 * n + 512)
                total = dot(dqkv[span, :], w[:, :, :, at].reshape(768, 512))
                ngs[first : first + chips // 2, :, at] = total.astype(BF).reshape(chips // 2, 32, 512)

        phase("back_project", back_project)
        copies = [
            remote(ngs.at[d], rs.at[d], rss.at[d], rsr.at[d], row, 2 * ((chip + chips - d) % chips) + core)
            for d in range(max(first, 1), first + chips // 2)
        ]
        for copy in copies:
            copy.start()
        scatter += copies
    def row_of(stat, p):
        return jnp.concatenate([stat[2 * p : 2 * p + 1], stat[2 * p + 1 : 2 * p + 2]], 1)

    for copy in rim_queries:
        copy.wait_recv()

    def rim_weights():
        terms = qh[:, 768:896].astype(F32).T
        rim_lse = terms[0:16] + terms[16:32] + terms[32:48]
        for p in range(6):
            at = 128 * p
            scores = dot_nt(slab[0:OWN, at : at + 128], both_heads(qh[:, at : at + 128] * SCALE)) + hbias[...]
            prim[p] = jnp.exp(scores - row_of(rim_lse, p)).astype(BF)

    phase("rim_weights", rim_weights)
    for copy in scatter:
        copy.wait_recv()

    def unmerge():
        total = ngs[0].astype(F32)
        for d in range(1, chips):
            total = total + rs[d].astype(F32)
        wide = jnp.concatenate([nb[0, 0], nb[1, 0]], 1).astype(F32)
        inverse = lax.rsqrt(jnp.mean(wide * wide, -1, keepdims=True) + 1e-06)
        scaled = total * gain
        cgrad = inverse * (scaled - wide * (inverse * inverse * jnp.mean(scaled * wide, -1, keepdims=True)))
        cgrad = cgrad.astype(BF)

        for n in range(3):
            at = slice(1024 * n, 1024 * n + 1024)
            mg[at, :] = dot_nt(mw[at, :], cgrad).astype(BF)
        token, t = iotas((128, 32))
        total = jnp.zeros((128, 768), F32)
        for s in range(4):
            total = total + dot_nt(pick(merge_token(32 * s + t), token), mg[768 * s : 768 * s + 768, :])
        amsg[:, 0:768] = total.astype(BF)
        product = amsg[:, 0:768].astype(F32) * attf[...]
        feature, lane_of = iotas((768, 128))
        heads = jnp.where(lane_of < 32, pick(feature >> 6, lane_of & 15).astype(F32), 0.0).astype(BF)
        high = product.astype(BF)
        delta = dot(high, heads) + dot((product - high.astype(F32)).astype(BF), heads)
        high = delta.astype(BF).astype(F32)
        amsg[:, 768:896] = jnp.where(lanes < 16, high, delta - high).astype(BF)
        i, t = iotas((128, 128))
        apack[...] = dot(pick(pack_token(i), t), amsg[...]).astype(BF)

    phase("unmerge", unmerge)

    rim_grads = to_neighbours(lambda at: amsg.at[pl.ds(at, 48)], apack, halo_rows(ah), gs, grs)
    for copy in rim_grads:
        copy.start()
    for copy in out_copies:
        copy.start()

    def fine_backward_own():
        for p in range(6):
            at = 128 * p
            query = both_heads(fine[:, at : at + 128] * SCALE)
            grad = both_heads(amsg[:, at : at + 128])
            weights_low = probs[p]
            weights = weights_low.astype(F32)
            dp = dot_nt(slab[:, 768 + at : 768 + at + 128], grad)
            delta = jnp.sum(weights * dp, 0, keepdims=True)
            ds_low = (weights * (dp - delta)).astype(BF)
            gown[:, at : at + 128] = dot(ds_low[0:OWN], query)
            gown[:, 768 + at : 768 + at + 128] = dot(weights_low[0:OWN], grad)
            dq = dot_tn(ds_low, slab[:, at : at + 128]) * SCALE
            fg_out[:, at : at + 128] = own_lanes(dq).astype(BF)

    phase("fine_back_own", fine_backward_own)

    dq_columns = pl.ds(0, 768)
    store_dq = pltpu.make_async_copy(fg_out.at[:, dq_columns], fg_hbm.at[:, dq_columns], dq_sem)
    store_dq.start()

    for d in range(1, chips):
        source = (chip + d) % chips
        remote(osend.at[d], corecv.at[source], os_.at[d], orr.at[d], row, 2 * source + core).wait_recv()

    def coarse_output():
        for c in range(chips):
            co_out[:, 128 * c : 128 * c + 128] = corecv[c, :, 0:128]
        for c in range(0, chips, 2):
            at = 1024 + 64 * c
            co_out[:, at : at + 128] = jnp.concatenate([corecv[c, :, 128:192], corecv[c + 1, :, 128:192]], 1)

    phase("coarse_output", coarse_output)
    store_co = pltpu.make_async_copy(co_out, co_hbm, co_sem)
    store_co.start()
    for copy in rim_grads:
        copy.wait_recv()

    def fine_backward_rim():
        terms = ah[:, 768:896].astype(F32).T
        rim_delta = terms[0:16] + terms[16:32]

        for p in range(6):
            at, val = 128 * p, 768 + 128 * p
            query = both_heads(qh[:, at : at + 128] * SCALE)
            grad = both_heads(ah[:, at : at + 128])
            weights_low = prim[p]
            weights = weights_low.astype(F32)
            dp = dot_nt(slab[0:OWN, val : val + 128], grad)
            ds_low = (weights * (dp - row_of(rim_delta, p))).astype(BF)
            dk = gown[:, at : at + 128] + dot(ds_low, query)
            dv = gown[:, val : val + 128] + dot(weights_low, grad)
            fg_out[:, 768 + at : 896 + at] = dk.astype(BF)
            fg_out[:, 768 + val : 896 + val] = dv.astype(BF)

    phase("fine_back_rim", fine_backward_rim)
    stores = [store_dq, store_co]
    for n in range(2):
        columns = pl.ds(768 + 768 * n, 768)
        stores.append(pltpu.make_async_copy(fg_out.at[:, columns], fg_hbm.at[:, columns], kv_sem.at[n]))
        stores[-1].start()
    for copy in halo + cot_copies + gather[0] + gather[1] + [swap_k, swap_v, swap_d] + out_copies + scatter + rim_queries + rim_grads:
        copy.wait_send()
    for away, copy in chunks:

        @pl.when(away)
        def _():
            copy.wait_send()

    def sent_along_y(n):
        for copy in along_y(n):
            copy.wait_send()

    each_part(core, range(4), lambda n: to_partner(n).wait_send())
    each_part(core, [low_row], sent_along_y)
    for store in stores:
        store.wait()


def carry(a, b, a_out, b_out):
    a_out[...] = a[...]
    b_out[...] = b[...]


def shards(mesh_rows, mesh_cols, fine_qkv, merge_weight, coarse_weight, norm_gain, cotangent):
    chips = mesh_cols // 2
    tokens = 32 * chips
    vmem = pl.BlockSpec(memory_space=pltpu.VMEM)
    hbm = pl.BlockSpec(memory_space=pl.ANY)
    dma = pltpu.SemaphoreType.DMA

    def low(*shape):
        return pltpu.VMEM(shape, BF)

    def full(*shape):
        return pltpu.VMEM(shape, F32)

    coarse_out, fine_grad = pl.pallas_call(
        functools.partial(kernel, mesh_rows, mesh_cols),
        out_shape=(jax.ShapeDtypeStruct((32, 1536), BF), jax.ShapeDtypeStruct((128, 2304), BF)),
        in_specs=[hbm] * 5,
        out_specs=(hbm, hbm),
        scratch_shapes=[
            low(32, 1536), low(128, 2304), low(128, 2304), low(32, 1536), full(1536), low(3072, 1536), low(SLAB, 1536), low(128, 1536), full(SLAB, 256),
            full(128, 512), low(6, SLAB, 256), low(6, 128, 512),
            full(16, 128), full(128, 768), low(128, 768),
            low(128, 896), low(128, 896), low(128, 896), low(128, 896), low(256, 896), low(256, 896),
            low(3, 8, 32, 1536), low(2, chips, 32, 768), low(tokens, 1536),
            low(chips, 32, 256), low(chips, 32, 256), low(tokens, 256), low(2 * tokens, 256),
            low(2 * tokens, 256), low(3, 2 * tokens, tokens), low(3, 2 * tokens, tokens), low(2, tokens, 256), low(2, tokens, 256), low(tokens, 768),
            low(chips, 32, 256), low(chips, 32, 256),
            low(chips, 32, 1536), low(chips, 32, 1536), low(3072, 32), full(128, 1536),
            dma, dma, dma, dma, dma, dma, dma((2,)), dma((8,)), dma((8,)), dma((8,)), dma((8,)), dma((8,)), dma((8,)), dma((9,)), dma((18,)),
            dma((18, 3)), dma((18,)), dma((2, chips)), dma((2, chips)), dma((chips,)), dma((chips,)),
            dma((2,)), dma((2,)), dma, dma, dma((chips,)), dma((chips,)), dma((chips,)), dma((chips,)),
        ],
        compiler_params=pltpu.CompilerParams(
            collective_id=0, has_side_effects=True, vmem_limit_bytes=56 * 1024 * 1024
        ),
    )(
        fine_qkv.reshape(128, 2304),
        merge_weight,
        coarse_weight.T,
        norm_gain,
        cotangent.reshape(32, 1536),
    )
    coarse_out, fine_grad = pl.pallas_call(
        carry,
        out_shape=(jax.ShapeDtypeStruct((32, 1536), BF), jax.ShapeDtypeStruct((128, 2304), BF)),
        in_specs=[vmem, vmem],
        out_specs=(vmem, vmem),
    )(coarse_out, fine_grad)
    return coarse_out.reshape(4, 8, 1536), fine_grad.reshape(8, 16, 2304)


def solution(mesh):
    placed = (P("row", "col", None), P(), P(None, "col"), P(), P("row", "col", None))
    return jax.shard_map(
        functools.partial(shards, mesh.shape["row"], mesh.shape["col"]),
        mesh=mesh,
        in_specs=placed,
        out_specs=(P("row", "col", None), P("row", "col", None)),
        check_vma=False,
    )
```
